256 devices in a mesh: row: 32 (over x_hi, z, core), col: 8 (over x_lo, y).
Axes of the slice: x: 4 (x_hi: 2, x_lo: 2; x = x_hi * 2 + x_lo), y: 4, z: 8, core: 2. Of those that a mesh axis runs over, the one named last changes fastest.
Arguments:
- regions: bfloat16 [16384, 256], P(('row', 'col')), may hold values from -1.25 to 1.25
- phrases: bfloat16 [16384, 256], P(('row', 'col')), may hold values from -1.25 to 1.25
Outputs:
- grad_regions: float32 [16384, 256], P(('row', 'col'))
- grad_phrases: float32 [16384, 256], P(('row', 'col'))
- divergence: float32 [], replicated
The draws below stay inside these ranges and needn't reach their ends.
All inputs are finite; a program needn't handle non-finite values.
Results may differ from the reference program's by a relative error of at most 0.0035.
Values may be sent and summed in bfloat16 or wider, within the bound.
No kernel may reach another device: no remote copies, remote signals or barrier semaphores. Data moves between devices by JAX's collectives and lax.ppermute only.
A program may use at most 64 MiB of HBM per device.

```python
import math
import jax
import jax.numpy as jnp
from jax import lax

D = 256
ITERS = 2
NPTS = 16384


def draw_regions(key, part):
    key = jax.random.fold_in(key, 1)
    jitter_key, scale_key = jax.random.split(key)
    jitter = jnp.clip(jax.random.normal(jitter_key, (NPTS, D), jnp.float32), -3.0, 3.0) / math.sqrt(D)
    scales = 0.4 * 10.0 ** jax.random.uniform(scale_key, (NPTS, 1), jnp.float32)
    values = jitter * scales
    return jnp.clip(values, -1.25, 1.25).astype(jnp.bfloat16)


def draw_phrases(key, part):
    key = jax.random.fold_in(key, 2)
    jitter_key, scale_key = jax.random.split(key)
    jitter = jnp.clip(jax.random.normal(jitter_key, (NPTS, D), jnp.float32), -3.0, 3.0) / math.sqrt(D)
    scales = 0.4 * 10.0 ** jax.random.uniform(scale_key, (NPTS, 1), jnp.float32)
    values = jitter * scales
    return jnp.clip(values, -1.25, 1.25).astype(jnp.bfloat16)


def setup_inputs(seed: int = 0) -> dict:
    splits = jax.random.split(jax.random.key(seed), 3)
    return {
        "regions": draw_regions(jax.random.fold_in(splits[2], 71), 0),
        "phrases": draw_phrases(jax.random.fold_in(splits[2], 71), 0),
    }


epsilon = 0.1


def half_square(points):
    values = points.astype(jnp.float32)
    return 0.5 * jnp.sum(values * values, axis=1)


def row_blocks(points):
    size_rows = min(512, points.shape[0])
    return points.reshape(points.shape[0] // size_rows, size_rows, points.shape[1])


def soft_rows(rows_emb, columns, col_shift):
    def one_block(block_rows):
        scores = col_shift[None, :] + jnp.dot(block_rows, columns.T, preferred_element_type=jnp.float32) / epsilon
        highest = jnp.max(scores, axis=1)
        return highest + jnp.log(jnp.sum(jnp.exp(scores - highest[:, None]), axis=1))

    return lax.map(one_block, row_blocks(rows_emb)).reshape(-1)


def soft_update(rows_emb, columns, potential, row_norms, col_norms):
    log_count = math.log(NPTS)
    return row_norms + epsilon * log_count - epsilon * soft_rows(rows_emb, columns, (potential - col_norms) / epsilon)


def row_term(rows_emb, columns, row_shift, col_shift):
    log_count = math.log(NPTS)

    def one_block(block_pair):
        block_rows, block_shift = block_pair
        products = jnp.dot(block_rows, columns.T, preferred_element_type=jnp.float32) / epsilon
        weights = jnp.exp(block_shift[:, None] + col_shift[None, :] + products - log_count)
        masses = jnp.sum(weights, axis=1)
        mixed_rows = jnp.dot(weights.astype(jnp.bfloat16), columns, preferred_element_type=jnp.float32)
        return block_rows.astype(jnp.float32) * masses[:, None] - mixed_rows

    blocks = row_blocks(rows_emb)
    shifts = row_shift.reshape(blocks.shape[0], blocks.shape[1])
    return lax.map(one_block, (blocks, shifts)).reshape(rows_emb.shape[0], rows_emb.shape[1])


def reference(regions, phrases):
    norm_x = half_square(regions)
    norm_y = half_square(phrases)
    cross_g = jnp.zeros((NPTS,), jnp.float32)
    self_p = jnp.zeros((NPTS,), jnp.float32)
    self_q = jnp.zeros((NPTS,), jnp.float32)
    for sweep_index in range(ITERS):
        cross_f = soft_update(regions, phrases, cross_g, norm_x, norm_y)
        cross_g = soft_update(phrases, regions, cross_f, norm_y, norm_x)
        fresh_p = soft_update(regions, regions, self_p, norm_x, norm_x)
        fresh_q = soft_update(phrases, phrases, self_q, norm_y, norm_y)
        if sweep_index == 0:
            self_p = fresh_p
            self_q = fresh_q
        else:
            self_p = 0.5 * (self_p + fresh_p)
            self_q = 0.5 * (self_q + fresh_q)
    divergence = jnp.mean(cross_f - self_p) + jnp.mean(cross_g - self_q)
    shift_u = (cross_f - norm_x) / epsilon
    shift_h = (cross_g - norm_y) / epsilon
    shift_p = (self_p - norm_x) / epsilon
    shift_q = (self_q - norm_y) / epsilon
    grad_regions = row_term(regions, phrases, shift_u, shift_h) - row_term(regions, regions, shift_p, shift_p)
    grad_phrases = row_term(phrases, regions, shift_h, shift_u) - row_term(phrases, phrases, shift_q, shift_q)
    return grad_regions, grad_phrases, divergence
```

```python
import math

import jax
import jax.numpy as jnp
from jax import lax
from jax.experimental import pallas as pl
from jax.experimental.pallas import tpu as pltpu
from jax.sharding import Mesh
from jax.sharding import PartitionSpec as P

EPSILON = 0.1
POINTS = 16384
OWN = 64
WIDTH = 256
HALF = 512
BLOCK = 1024
LOG_COUNT = math.log2(POINTS)
BETA = 1.0 / (EPSILON * math.log(2.0))
INV_LN2 = 1.0 / math.log(2.0)

AXES = ("xh", "z", "core", "xl", "y")
ROW_GROUP = ("core", "xl", "y")
COL_GROUP = ("xh", "z")

VMEM_LIMIT = 32 * 1024 * 1024


def log2(values):
    return jnp.log(values) * INV_LN2


def dot_nt(left, right):
    return lax.dot_general(left, right, (((1,), (1,)), ((), ())), preferred_element_type=jnp.float32)


def dense_to_sub(values):
    pieces = [jnp.broadcast_to(values[t : t + 1, :], (128, 128)).T for t in range(8)]
    return jnp.concatenate(pieces, axis=0)


def dense_to_lane(values):
    return jnp.concatenate([values[t : t + 1, :] for t in range(8)], axis=1)


def lane_to_dense(values):
    return jnp.concatenate([values[:, t * 128 : (t + 1) * 128] for t in range(8)], axis=0)


def widen(sub, lanes):
    return jnp.concatenate([sub] * (lanes // 128), axis=1)


def block_rows(own, other, which):
    parts = [ref[:, which * OWN : (which + 1) * OWN, :].reshape(HALF, WIDTH) for ref in (own, other)]
    return jnp.concatenate(parts, axis=0)


def quarter_rows(own, other, which, quarter):
    ref = own if quarter < 2 else other
    start = (quarter % 2) * 4
    return ref[start : start + 4, which * OWN : (which + 1) * OWN, :].reshape(256, WIDTH)


def half_rows(ref, which):
    return ref[:, which * OWN : (which + 1) * OWN, :].reshape(HALF, WIDTH)


def squares_split(rows):
    values = rows.astype(jnp.float32)
    squares = values * values
    high = squares.astype(jnp.bfloat16)
    low = (squares - high.astype(jnp.float32)).astype(jnp.bfloat16)
    return high, low


def norms_sub(rows):
    high, low = squares_split(rows)
    ones = jnp.ones((WIDTH, 128), jnp.bfloat16)
    total = jnp.dot(high, ones, preferred_element_type=jnp.float32) + jnp.dot(
        low, ones, preferred_element_type=jnp.float32
    )
    return total * (0.5 * BETA)


def norms_lane(rows):
    high, low = squares_split(rows)
    ones = jnp.ones((8, WIDTH), jnp.bfloat16)
    total = dot_nt(ones, high) + dot_nt(ones, low)
    return total[0:1, :] * (0.5 * BETA)


def sum_pass(reduced, own, other, which, sub, lane):
    outs = []
    wide = widen(sub, 256)
    for quarter in range(4):
        products = dot_nt(reduced, quarter_rows(own, other, which, quarter))
        part = lane[:, quarter * 256 : (quarter + 1) * 256]
        outs.append(jnp.sum(jnp.exp2(products * BETA + wide + part), axis=0, keepdims=True))
    return lane_to_dense(jnp.concatenate(outs, axis=1))


def peak_pass(reduced, own, other, which, sub):
    outs = []
    wide = widen(sub, 256)
    for quarter in range(4):
        products = dot_nt(reduced, quarter_rows(own, other, which, quarter))
        scores = products * BETA + wide
        peak = jnp.max(scores, axis=0, keepdims=True)
        mass = jnp.sum(jnp.exp2(scores - peak), axis=0, keepdims=True)
        outs.append(peak + log2(mass))
    return lane_to_dense(jnp.concatenate(outs, axis=1))


def swap_halves(values):
    return jnp.concatenate([values[4:8], values[0:4]], axis=0)


def peer_halves(ref, place, offset):
    mine = ref[pl.ds(place * 8, 8), offset : offset + 8, :]
    theirs = ref[pl.ds((1 - place) * 8, 8), offset : offset + 8, :]
    return mine, theirs


def join_sums(ref, place, offset):
    mine, theirs = peer_halves(ref, place, offset)
    return jnp.sum(mine, axis=0) + swap_halves(jnp.sum(theirs, axis=0))


def join_logs(ref, place, offset):
    mine, theirs = peer_halves(ref, place, offset)
    peak = jnp.maximum(jnp.max(mine, axis=0), swap_halves(jnp.max(theirs, axis=0)))
    other_peak = swap_halves(peak)
    mass = jnp.sum(jnp.exp2(mine - peak[None]), axis=0) + swap_halves(
        jnp.sum(jnp.exp2(theirs - other_peak[None]), axis=0)
    )
    return peak + log2(mass)


def lane_index():
    return lax.broadcasted_iota(jnp.int32, (1, 128), 1)


def own_piece(dense, place):
    row = jnp.zeros((1, 128), jnp.float32)
    for k in range(4):
        row = jnp.where(place // 2 == k, dense[k : k + 1, :], row)
    return jnp.where(place % 2 == 0, row, pltpu.roll(row, 64, 1))


def pair_row(first, second):
    return jnp.where(lane_index() < 64, first, pltpu.roll(second, 64, 1))


def piggy_rows(ref, place, row):
    order = []
    for base in (place * 8, (1 - place) * 8):
        for k in range(8):
            order.append(ref[base + k, row : row + 1, :])
    even = jnp.concatenate(order[0::2], axis=0)
    odd = jnp.concatenate(order[1::2], axis=0)
    return even, odd


def unpair(even, odd):
    lane = lax.broadcasted_iota(jnp.int32, (8, 128), 1)
    first = jnp.where(lane < 64, even, pltpu.roll(odd, 64, 1))
    second = jnp.where(lane < 64, pltpu.roll(even, 64, 1), odd)
    return first, second


def canonical_sum(values):
    return jnp.sum(values[0:4], keepdims=True) + jnp.sum(values[4:8], keepdims=True)


def send_all(message_ref, rows):
    message_ref[...] = jnp.broadcast_to(rows[None], message_ref.shape)


def first_rows(r_own, r_other, c_own, c_other, message, norms):
    x_col = block_rows(c_own, c_other, 0)
    y_col = block_rows(c_own, c_other, 1)
    x_norm_sub = norms_sub(x_col)
    y_norm_sub = norms_sub(y_col)
    x_norm = norms_lane(block_rows(r_own, r_other, 0))
    y_norm = norms_lane(block_rows(r_own, r_other, 1))
    cross = peak_pass(y_col, r_own, r_other, 0, -y_norm_sub)
    self_p = sum_pass(x_col, r_own, r_other, 0, -x_norm_sub, -x_norm)
    self_q = sum_pass(y_col, r_own, r_other, 1, -y_norm_sub, -y_norm)
    send_all(message, jnp.concatenate([cross, self_p, self_q], axis=0))
    x_norm_col = norms_lane(x_col)
    y_norm_col = norms_lane(y_col)
    norms[...] = jnp.concatenate(
        [lane_to_dense(v) for v in (x_norm, y_norm, x_norm_col, y_norm_col)], axis=0
    )


def first_cols(place, r_own, r_other, c_own, c_other, got, message, state):
    core, spot = place[0], place[1]
    u = LOG_COUNT - join_logs(got, core, 0)
    p = LOG_COUNT - log2(join_sums(got, core, 8))
    q = LOG_COUNT - log2(join_sums(got, core, 16))
    x_row = block_rows(r_own, r_other, 0)
    cross = peak_pass(x_row, c_own, c_other, 1, dense_to_sub(u))
    carry = pair_row(own_piece(p, spot), own_piece(q, spot))
    send_all(message, jnp.concatenate([cross, jnp.broadcast_to(carry, (8, 128))], axis=0))
    state[...] = jnp.concatenate([u, p, q], axis=0)


def second_rows(place, r_own, r_other, c_own, c_other, norms, state, got, message, h_out):
    far = place[2]
    h = LOG_COUNT - join_logs(got, far, 0)
    p_col, q_col = unpair(*piggy_rows(got, far, 8))
    x_col = block_rows(c_own, c_other, 0)
    y_col = block_rows(c_own, c_other, 1)
    cross = sum_pass(y_col, r_own, r_other, 0, dense_to_sub(h), dense_to_lane(state[0:8, :]))
    self_p = sum_pass(
        x_col, r_own, r_other, 0, dense_to_sub(p_col - norms[16:24, :]), -dense_to_lane(norms[0:8, :])
    )
    self_q = sum_pass(
        y_col, r_own, r_other, 1, dense_to_sub(q_col - norms[24:32, :]), -dense_to_lane(norms[8:16, :])
    )
    send_all(message, jnp.concatenate([cross, self_p, self_q], axis=0))
    h_out[...] = h


def second_cols(place, r_own, r_other, c_own, c_other, norms, state, h_in, got, message, shifts):
    core, spot = place[0], place[1]
    u = state[0:8, :] + (LOG_COUNT - log2(join_sums(got, core, 0)))
    p = 0.5 * (state[8:16, :] + (LOG_COUNT - log2(join_sums(got, core, 8))))
    q = 0.5 * (state[16:24, :] + (LOG_COUNT - log2(join_sums(got, core, 16))))
    pt = p - norms[0:8, :]
    qt = q - norms[8:16, :]
    x_row = block_rows(r_own, r_other, 0)
    cross = sum_pass(x_row, c_own, c_other, 1, dense_to_sub(u), dense_to_lane(h_in[...]))
    first = pair_row(own_piece(u, spot), own_piece(pt, spot))
    second = pair_row(own_piece(qt, spot), jnp.zeros((1, 128), jnp.float32))
    total = jnp.broadcast_to(canonical_sum(u - pt - qt), (6, 128))
    send_all(message, jnp.concatenate([cross, first, second, total], axis=0))
    shifts[...] = jnp.concatenate([u, pt, qt], axis=0)


def last_cols(place, h_in, got, message, cols, total):
    far, spot = place[2], place[3]
    h = h_in[...] + (LOG_COUNT - log2(join_sums(got, far, 0)))
    u_col, p_col = unpair(*piggy_rows(got, far, 8))
    q_col, unused = unpair(*piggy_rows(got, far, 9))
    piece = own_piece(h, spot)
    part = jnp.broadcast_to(canonical_sum(h), (7, 128))
    send_all(message, jnp.concatenate([piece, part], axis=0))
    cols[...] = jnp.concatenate([h, u_col, p_col, q_col], axis=0)
    total[...] = jnp.sum(got[:, 8:16, :], axis=0)


def gradients(place, r_own, r_other, c_own, c_other, shifts, cols, total, got, kept, sent, divergence):
    core = place[0]
    h_row, unused = unpair(*piggy_rows(got, core, 0))
    summed = total[...] + jnp.sum(got[...], axis=0)
    divergence[...] = summed * (1.0 / (POINTS * BETA))
    u_sub = dense_to_sub(shifts[0:8, :])
    p_sub = dense_to_sub(shifts[8:16, :])
    q_sub = dense_to_sub(shifts[16:24, :])
    h_sub = dense_to_sub(h_row)
    h_lane, u_lane, p_lane, q_lane = [
        dense_to_lane(cols[8 * k : 8 * k + 8, :]) - LOG_COUNT for k in range(4)
    ]
    x_col = block_rows(c_own, c_other, 0)
    y_col = block_rows(c_own, c_other, 1)

    def weights(rows, columns, sub, lane):
        products = dot_nt(rows, columns)
        values = jnp.exp2(products * BETA + widen(sub, BLOCK) + lane)
        mass = jnp.sum(values, axis=1, keepdims=True)
        mixed = jnp.dot(values.astype(jnp.bfloat16), columns, preferred_element_type=jnp.float32)
        return mass, mixed

    for ref, out, start in ((r_other, sent, HALF), (r_own, kept, 0)):
        part = slice(start, start + HALF)
        for which, cross_col, self_col, cross_sub, self_sub, cross_lane, self_lane in (
            (0, y_col, x_col, u_sub, p_sub, h_lane, p_lane),
            (1, x_col, y_col, h_sub, q_sub, u_lane, q_lane),
        ):
            rows = half_rows(ref, which)
            cross_mass, cross_mixed = weights(rows, cross_col, cross_sub[part], cross_lane)
            self_mass, self_mixed = weights(rows, self_col, self_sub[part], self_lane)
            grad = rows.astype(jnp.float32) * (cross_mass - self_mass) - cross_mixed + self_mixed
            out[:, which * OWN : (which + 1) * OWN, :] = grad.reshape(8, OWN, WIDTH).astype(out.dtype)


def call(body, outs, smem, *args):
    shapes = [jax.ShapeDtypeStruct(shape, dtype) for shape, dtype in outs]
    specs = [pl.BlockSpec(memory_space=pltpu.VMEM)] * len(args)
    if smem:
        specs[0] = pl.BlockSpec(memory_space=pltpu.SMEM)
    return pl.pallas_call(
        body,
        out_shape=shapes,
        in_specs=specs,
        out_specs=[pl.BlockSpec(memory_space=pltpu.VMEM)] * len(outs),
        compiler_params=pltpu.CompilerParams(vmem_limit_bytes=VMEM_LIMIT),
    )(*args)


def share(message, axes):
    return lax.all_to_all(message, axes, 0, 0, tiled=True)


def on_device(regions, phrases):
    f32 = jnp.float32
    core = lax.axis_index("core")
    spot_row = lax.axis_index("xl") * 4 + lax.axis_index("y")
    far = lax.axis_index("xh")
    spot_col = lax.axis_index("z")
    place = jnp.stack([core, spot_row, far, spot_col]).astype(jnp.int32)

    own = jnp.concatenate([regions, phrases], axis=0)
    copies = jnp.broadcast_to(own[None], (8, 2 * OWN, WIDTH))
    c_own = share(copies, ("z",))
    c_other = lax.ppermute(c_own, "xh", [(0, 1), (1, 0)])
    r_own = share(copies, ("xl", "y"))
    r_other = lax.ppermute(r_own, "core", [(0, 1), (1, 0)])
    points = (r_own, r_other, c_own, c_other)

    def message(rows):
        return ((16, rows, 128), f32)

    sent, norms = call(first_rows, [message(24), ((32, 128), f32)], False, *points)
    got = share(sent, ROW_GROUP)
    sent, state = call(first_cols, [message(16), ((24, 128), f32)], True, place, *points, got)
    got = share(sent, COL_GROUP)
    sent, h_first = call(
        second_rows, [message(24), ((8, 128), f32)], True, place, *points, norms, state, got
    )
    got = share(sent, ROW_GROUP)
    sent, shifts = call(
        second_cols, [message(16), ((24, 128), f32)], True, place, *points, norms, state, h_first, got
    )
    got = share(sent, COL_GROUP)
    sent, cols, total = call(
        last_cols, [message(8), ((32, 128), f32), ((8, 128), f32)], True, place, h_first, got
    )
    got = share(sent, ROW_GROUP)
    kept, away, divergence = call(
        gradients,
        [((8, 2 * OWN, WIDTH), f32), ((8, 2 * OWN, WIDTH), f32), ((8, 128), f32)],
        True,
        place,
        *points,
        shifts,
        cols,
        total,
        got,
    )
    joined = kept + lax.ppermute(away, "core", [(0, 1), (1, 0)])
    summed = jnp.sum(share(joined, ("xl", "y")), axis=0)
    return (summed[0:OWN], summed[OWN : 2 * OWN], divergence[2, 0])


def solution(mesh):
    fine = Mesh(mesh.devices.reshape(2, 8, 2, 2, 4), AXES)
    return jax.shard_map(
        on_device,
        mesh=fine,
        in_specs=(P(AXES, None), P(AXES, None)),
        out_specs=(P(AXES, None), P(AXES, None), P()),
        check_vma=False,
    )
```

```python
import math

import jax
import jax.numpy as jnp
from jax import lax
from jax.experimental import pallas as pl
from jax.experimental.pallas import tpu as pltpu
from jax.sharding import Mesh
from jax.sharding import PartitionSpec as P

EPSILON = 0.1
POINTS = 16384
OWN = 64
WIDTH = 256
HALF = 512
BLOCK = 1024
LOG_COUNT = math.log2(POINTS)
BETA = 1.0 / (EPSILON * math.log(2.0))
INV_LN2 = 1.0 / math.log(2.0)

AXES = ("xh", "z", "core", "xl", "y")
ROW_GROUP = ("core", "xl", "y")

VMEM_LIMIT = 32 * 1024 * 1024


def log2(values):
    return jnp.log(values) * INV_LN2


def dot_nt(left, right):
    return lax.dot_general(left, right, (((1,), (1,)), ((), ())), preferred_element_type=jnp.float32)


def dense_to_sub(values):
    pieces = [jnp.broadcast_to(values[t : t + 1, :], (128, 128)).T for t in range(8)]
    return jnp.concatenate(pieces, axis=0)


def dense_to_lane(values):
    return jnp.concatenate([values[t : t + 1, :] for t in range(8)], axis=1)


def lane_to_dense(values):
    return jnp.concatenate([values[:, t * 128 : (t + 1) * 128] for t in range(8)], axis=0)


def widen(sub, lanes):
    return jnp.concatenate([sub] * (lanes // 128), axis=1)


def block_rows(own, other, which):
    parts = [ref[:, which * OWN : (which + 1) * OWN, :].reshape(HALF, WIDTH) for ref in (own, other)]
    return jnp.concatenate(parts, axis=0)


def quarter_rows(own, other, which, quarter):
    ref = own if quarter < 2 else other
    start = (quarter % 2) * 4
    return ref[start : start + 4, which * OWN : (which + 1) * OWN, :].reshape(256, WIDTH)


def half_rows(ref, which):
    return ref[:, which * OWN : (which + 1) * OWN, :].reshape(HALF, WIDTH)


def squares_split(rows):
    values = rows.astype(jnp.float32)
    squares = values * values
    high = squares.astype(jnp.bfloat16)
    low = (squares - high.astype(jnp.float32)).astype(jnp.bfloat16)
    return high, low


def norms_sub(rows):
    high, low = squares_split(rows)
    ones = jnp.ones((WIDTH, 128), jnp.bfloat16)
    total = jnp.dot(high, ones, preferred_element_type=jnp.float32) + jnp.dot(
        low, ones, preferred_element_type=jnp.float32
    )
    return total * (0.5 * BETA)


def norms_lane(rows):
    high, low = squares_split(rows)
    ones = jnp.ones((8, WIDTH), jnp.bfloat16)
    total = dot_nt(ones, high) + dot_nt(ones, low)
    return total[0:1, :] * (0.5 * BETA)


def sum_pass(reduced, own, other, which, sub, lane):
    outs = []
    wide = widen(sub, 256)
    for quarter in range(4):
        products = dot_nt(reduced, quarter_rows(own, other, which, quarter))
        part = lane[:, quarter * 256 : (quarter + 1) * 256]
        outs.append(jnp.sum(jnp.exp2(products * BETA + wide + part), axis=0, keepdims=True))
    return lane_to_dense(jnp.concatenate(outs, axis=1))


def peak_pass(reduced, own, other, which, sub):
    outs = []
    wide = widen(sub, 256)
    for quarter in range(4):
        products = dot_nt(reduced, quarter_rows(own, other, which, quarter))
        scores = products * BETA + wide
        peak = jnp.max(scores, axis=0, keepdims=True)
        mass = jnp.sum(jnp.exp2(scores - peak), axis=0, keepdims=True)
        outs.append(peak + log2(mass))
    return lane_to_dense(jnp.concatenate(outs, axis=1))


def swap_halves(values):
    return jnp.concatenate([values[4:8], values[0:4]], axis=0)


def peer_halves(ref, place, offset):
    mine = ref[pl.ds(place * 8, 8), offset : offset + 8, :]
    theirs = ref[pl.ds((1 - place) * 8, 8), offset : offset + 8, :]
    return mine, theirs


def join_sums(ref, place, offset):
    mine, theirs = peer_halves(ref, place, offset)
    return jnp.sum(mine, axis=0) + swap_halves(jnp.sum(theirs, axis=0))


def join_logs(ref, place, offset):
    mine, theirs = peer_halves(ref, place, offset)
    peak = jnp.maximum(jnp.max(mine, axis=0), swap_halves(jnp.max(theirs, axis=0)))
    other_peak = swap_halves(peak)
    mass = jnp.sum(jnp.exp2(mine - peak[None]), axis=0) + swap_halves(
        jnp.sum(jnp.exp2(theirs - other_peak[None]), axis=0)
    )
    return peak + log2(mass)


def lane_index():
    return lax.broadcasted_iota(jnp.int32, (1, 128), 1)


def own_piece(dense, place):
    row = jnp.zeros((1, 128), jnp.float32)
    for k in range(4):
        row = jnp.where(place // 2 == k, dense[k : k + 1, :], row)
    return jnp.where(place % 2 == 0, row, pltpu.roll(row, 64, 1))


def pair_row(first, second):
    return jnp.where(lane_index() < 64, first, pltpu.roll(second, 64, 1))


def piggy_rows(ref, place, row):
    order = []
    for base in (place * 8, (1 - place) * 8):
        for k in range(8):
            order.append(ref[base + k, row : row + 1, :])
    even = jnp.concatenate(order[0::2], axis=0)
    odd = jnp.concatenate(order[1::2], axis=0)
    return even, odd


def unpair(even, odd):
    lane = lax.broadcasted_iota(jnp.int32, (8, 128), 1)
    first = jnp.where(lane < 64, even, pltpu.roll(odd, 64, 1))
    second = jnp.where(lane < 64, pltpu.roll(even, 64, 1), odd)
    return first, second


def canonical_sum(values):
    return jnp.sum(values[0:4], keepdims=True) + jnp.sum(values[4:8], keepdims=True)


def send_all(message_ref, rows):
    message_ref[...] = jnp.broadcast_to(rows[None], message_ref.shape)


def first_rows(r_own, r_other, c_own, c_other, message):
    y_col = block_rows(c_own, c_other, 1)
    send_all(message, peak_pass(y_col, r_own, r_other, 0, -norms_sub(y_col)))


def first_self(r_own, r_other, c_own, c_other, sums, norms):
    x_row = block_rows(r_own, r_other, 0)
    y_row = block_rows(r_own, r_other, 1)
    x_norm_col = norms_lane(block_rows(c_own, c_other, 0))
    y_norm_col = norms_lane(block_rows(c_own, c_other, 1))
    self_p = sum_pass(x_row, c_own, c_other, 0, -norms_sub(x_row), -x_norm_col)
    self_q = sum_pass(y_row, c_own, c_other, 1, -norms_sub(y_row), -y_norm_col)
    sums[...] = jnp.concatenate([self_p, self_q], axis=0)
    norms[...] = jnp.concatenate(
        [lane_to_dense(v) for v in (norms_lane(x_row), norms_lane(y_row), x_norm_col, y_norm_col)],
        axis=0,
    )


def first_cols(place, r_own, r_other, c_own, c_other, sums, got, message, state):
    u = LOG_COUNT - join_logs(got, place[0], 0)
    x_row = block_rows(r_own, r_other, 0)
    cross = peak_pass(x_row, c_own, c_other, 1, dense_to_sub(u))
    send_all(message, jnp.concatenate([cross, sums[...]], axis=0))
    state[...] = u


def second_rows(place, r_own, r_other, c_own, c_other, norms, state, got, message, h_out):
    far, spot = place[2], place[3]
    h = LOG_COUNT - join_logs(got, far, 0)
    p = LOG_COUNT - log2(join_sums(got, far, 8))
    q = LOG_COUNT - log2(join_sums(got, far, 16))
    x_col = block_rows(c_own, c_other, 0)
    y_col = block_rows(c_own, c_other, 1)
    cross = sum_pass(y_col, r_own, r_other, 0, dense_to_sub(h), dense_to_lane(state[...]))
    self_p = sum_pass(
        x_col, r_own, r_other, 0, dense_to_sub(p - norms[16:24, :]), -dense_to_lane(norms[0:8, :])
    )
    self_q = sum_pass(
        y_col, r_own, r_other, 1, dense_to_sub(q - norms[24:32, :]), -dense_to_lane(norms[8:16, :])
    )
    carry = jnp.broadcast_to(pair_row(own_piece(p, spot), own_piece(q, spot)), (8, 128))
    send_all(message, jnp.concatenate([cross, self_p, self_q, carry], axis=0))
    h_out[...] = h


def second_cols(place, r_own, r_other, c_own, c_other, norms, state, h_in, got, message, shifts):
    core, spot = place[0], place[1]
    p_first, q_first = unpair(*piggy_rows(got, core, 24))
    u = state[...] + (LOG_COUNT - log2(join_sums(got, core, 0)))
    p = 0.5 * (p_first + (LOG_COUNT - log2(join_sums(got, core, 8))))
    q = 0.5 * (q_first + (LOG_COUNT - log2(join_sums(got, core, 16))))
    pt = p - norms[0:8, :]
    qt = q - norms[8:16, :]
    x_row = block_rows(r_own, r_other, 0)
    cross = sum_pass(x_row, c_own, c_other, 1, dense_to_sub(u), dense_to_lane(h_in[...]))
    first = pair_row(own_piece(u, spot), own_piece(pt, spot))
    second = pair_row(own_piece(qt, spot), jnp.zeros((1, 128), jnp.float32))
    total = jnp.broadcast_to(canonical_sum(u - pt - qt), (6, 128))
    send_all(message, jnp.concatenate([cross, first, second, total], axis=0))
    shifts[...] = jnp.concatenate([u, pt, qt], axis=0)


def last_cols(place, h_in, got, message, cols, total):
    far, spot = place[2], place[3]
    h = h_in[...] + (LOG_COUNT - log2(join_sums(got, far, 0)))
    u_col, p_col = unpair(*piggy_rows(got, far, 8))
    q_col, unused = unpair(*piggy_rows(got, far, 9))
    piece = own_piece(h, spot)
    part = jnp.broadcast_to(canonical_sum(h), (7, 128))
    send_all(message, jnp.concatenate([piece, part], axis=0))
    cols[...] = jnp.concatenate([h, u_col, p_col, q_col], axis=0)
    total[...] = jnp.sum(got[:, 8:16, :], axis=0)


def weights(rows, columns, sub, lane):
    products = dot_nt(rows, columns)
    values = jnp.exp2(products * BETA + widen(sub, BLOCK) + lane)
    mass = jnp.sum(values, axis=1, keepdims=True)
    mixed = jnp.dot(values.astype(jnp.bfloat16), columns, preferred_element_type=jnp.float32)
    return mass, mixed


def gradient_half(ref, which, part, cross, self_):
    rows = half_rows(ref, which)
    cross_mass, cross_mixed = weights(rows, cross[0], cross[1][part], cross[2])
    self_mass, self_mixed = weights(rows, self_[0], self_[1][part], self_[2])
    grad = rows.astype(jnp.float32) * (cross_mass - self_mass) - cross_mixed + self_mixed
    return grad.reshape(8, OWN, WIDTH)


def col_lane(cols, k):
    return dense_to_lane(cols[8 * k : 8 * k + 8, :]) - LOG_COUNT


def region_gradients(r_own, r_other, c_own, c_other, shifts, cols, kept, sent):
    cross = (block_rows(c_own, c_other, 1), dense_to_sub(shifts[0:8, :]), col_lane(cols, 0))
    self_ = (block_rows(c_own, c_other, 0), dense_to_sub(shifts[8:16, :]), col_lane(cols, 2))
    sent[...] = gradient_half(r_other, 0, slice(HALF, BLOCK), cross, self_)
    kept[...] = gradient_half(r_own, 0, slice(0, HALF), cross, self_)


def phrase_gradients(
    place, r_own, r_other, c_own, c_other, shifts, cols, total, got, kept, sent, divergence
):
    h_row, unused = unpair(*piggy_rows(got, place[0], 0))
    summed = total[...] + jnp.sum(got[...], axis=0)
    divergence[...] = summed * (1.0 / (POINTS * BETA))
    cross = (block_rows(c_own, c_other, 0), dense_to_sub(h_row), col_lane(cols, 1))
    self_ = (block_rows(c_own, c_other, 1), dense_to_sub(shifts[16:24, :]), col_lane(cols, 3))
    sent[...] = gradient_half(r_other, 1, slice(HALF, BLOCK), cross, self_)
    kept[...] = gradient_half(r_own, 1, slice(0, HALF), cross, self_)


def call(body, outs, smem, passes, *args):
    shapes = [jax.ShapeDtypeStruct(shape, dtype) for shape, dtype in outs]
    specs = [pl.BlockSpec(memory_space=pltpu.VMEM)] * len(args)
    if smem:
        specs[0] = pl.BlockSpec(memory_space=pltpu.SMEM)
    return pl.pallas_call(
        body,
        out_shape=shapes,
        in_specs=specs,
        out_specs=[pl.BlockSpec(memory_space=pltpu.VMEM)] * len(outs),
        compiler_params=pltpu.CompilerParams(vmem_limit_bytes=VMEM_LIMIT),
        cost_estimate=pl.CostEstimate(
            flops=passes * 2 * BLOCK * BLOCK * WIDTH,
            bytes_accessed=4 * BLOCK * WIDTH * 2,
            transcendentals=passes * BLOCK * BLOCK,
        ),
    )(*args)


def share(message, axes, groups=None):
    return lax.all_to_all(message, axes, 0, 0, tiled=True, axis_index_groups=groups)


def share_col(message):
    groups = [
        [far * 16 + z * 2 + (side ^ far) for far in range(2) for z in range(8)] for side in range(2)
    ]
    return share(message, ("xh", "z", "xl"), groups)


def core_swap(values):
    return lax.ppermute(values, "core", [(0, 1), (1, 0)])


def on_device(regions, phrases):
    f32 = jnp.float32
    core = lax.axis_index("core")
    spot_row = lax.axis_index("xl") * 4 + lax.axis_index("y")
    far = lax.axis_index("xh")
    spot_col = lax.axis_index("z")
    place = jnp.stack([core, spot_row, far, spot_col]).astype(jnp.int32)

    own = jnp.concatenate([regions, phrases], axis=0)
    copies = jnp.broadcast_to(own[None], (8, 2 * OWN, WIDTH))
    c_own = share(copies, ("z",))
    c_own, copies = lax.optimization_barrier((c_own, copies))
    c_other = lax.ppermute(c_own, ("xh", "xl"), [(0, 3), (1, 2), (2, 1), (3, 0)])
    r_own = share(copies, ("xl", "y"))
    r_other = core_swap(r_own)
    points = (r_own, r_other, c_own, c_other)

    def message(rows):
        return ((16, rows, 128), f32)

    (sent,) = call(first_rows, [message(8)], False, 1, *points)
    later, sent = lax.optimization_barrier((points, sent))
    got = share(sent, ROW_GROUP)
    sums, norms = call(first_self, [((16, 128), f32), ((32, 128), f32)], False, 2, *later)
    sent, state = call(
        first_cols, [message(24), ((8, 128), f32)], True, 1, place, *points, sums, got
    )
    got = share_col(sent)
    sent, h_first = call(
        second_rows, [message(32), ((8, 128), f32)], True, 3, place, *points, norms, state, got
    )
    got = share(sent, ROW_GROUP)
    sent, shifts = call(
        second_cols,
        [message(16), ((24, 128), f32)],
        True,
        1,
        place,
        *points,
        norms,
        state,
        h_first,
        got,
    )
    got = share_col(sent)
    sent, cols, total = call(
        last_cols, [message(8), ((32, 128), f32), ((8, 128), f32)], True, 0, place, h_first, got
    )
    got = share(sent, ROW_GROUP)
    half = ((8, OWN, WIDTH), f32)
    x_kept, x_away = call(region_gradients, [half, half], False, 4, *points, shifts, cols)
    x_back = core_swap(x_away)
    y_kept, y_away, divergence = call(
        phrase_gradients,
        [half, half, ((8, 128), f32)],
        True,
        4,
        place,
        *points,
        shifts,
        cols,
        total,
        got,
    )
    y_back = core_swap(y_away)
    joined = jnp.concatenate([x_kept + x_back, y_kept + y_back], axis=1).astype(jnp.bfloat16)
    parts = share(joined, ("xl", "y")).astype(f32)
    summed = jnp.sum(parts, axis=0)
    return (summed[0:OWN], summed[OWN : 2 * OWN], divergence[2, 0])


def solution(mesh):
    fine = Mesh(mesh.devices.reshape(2, 8, 2, 2, 4), AXES)
    return jax.shard_map(
        on_device,
        mesh=fine,
        in_specs=(P(AXES, None), P(AXES, None)),
        out_specs=(P(AXES, None), P(AXES, None), P()),
        check_vma=False,
    )
```

```python
import math

import jax
import jax.numpy as jnp
from jax import lax
from jax.experimental import pallas as pl
from jax.experimental.pallas import tpu as pltpu
from jax.sharding import Mesh
from jax.sharding import PartitionSpec as P

EPSILON = 0.1
POINTS = 16384
OWN = 64
WIDTH = 256
HALF = 512
BLOCK = 1024
LOG_COUNT = math.log2(POINTS)
BETA = 1.0 / (EPSILON * math.log(2.0))
INV_LN2 = 1.0 / math.log(2.0)

AXES = ("xh", "z", "core", "xl", "y")
ROW_GROUP = ("core", "xl", "y")

VMEM_LIMIT = 20 * 1024 * 1024


def log2(values):
    return jnp.log(values) * INV_LN2


def dot_nt(left, right):
    return lax.dot_general(left, right, (((1,), (1,)), ((), ())), preferred_element_type=jnp.float32)


def dense_to_sub(values):
    pieces = [jnp.broadcast_to(values[t : t + 1, :], (128, 128)).T for t in range(8)]
    return jnp.concatenate(pieces, axis=0)


def dense_to_lane(values):
    return jnp.concatenate([values[t : t + 1, :] for t in range(8)], axis=1)


def lane_to_dense(values):
    return jnp.concatenate([values[:, t * 128 : (t + 1) * 128] for t in range(8)], axis=0)


def widen(sub, lanes):
    return jnp.concatenate([sub] * (lanes // 128), axis=1)


def block_rows(own, other, which):
    parts = [ref[:, which * OWN : (which + 1) * OWN, :].reshape(HALF, WIDTH) for ref in (own, other)]
    return jnp.concatenate(parts, axis=0)


def quarter_rows(own, other, which, quarter):
    ref = own if quarter < 2 else other
    start = (quarter % 2) * 4
    return ref[start : start + 4, which * OWN : (which + 1) * OWN, :].reshape(256, WIDTH)


def half_rows(ref, which):
    return ref[:, which * OWN : (which + 1) * OWN, :].reshape(HALF, WIDTH)


def squares_split(rows):
    values = rows.astype(jnp.float32)
    squares = values * values
    high = squares.astype(jnp.bfloat16)
    low = (squares - high.astype(jnp.float32)).astype(jnp.bfloat16)
    return high, low


def norms_sub(rows):
    high, low = squares_split(rows)
    ones = jnp.ones((WIDTH, 128), jnp.bfloat16)
    total = jnp.dot(high, ones, preferred_element_type=jnp.float32) + jnp.dot(
        low, ones, preferred_element_type=jnp.float32
    )
    return total * (0.5 * BETA)


def norms_lane(rows):
    high, low = squares_split(rows)
    ones = jnp.ones((8, WIDTH), jnp.bfloat16)
    total = dot_nt(ones, high) + dot_nt(ones, low)
    return total[0:1, :] * (0.5 * BETA)


def sum_pass(reduced, own, other, which, sub, lane):
    outs = []
    wide = widen(sub, 256)
    for quarter in range(4):
        products = dot_nt(reduced, quarter_rows(own, other, which, quarter))
        part = lane[:, quarter * 256 : (quarter + 1) * 256]
        outs.append(jnp.sum(jnp.exp2(products * BETA + wide + part), axis=0, keepdims=True))
    return lane_to_dense(jnp.concatenate(outs, axis=1))


def peak_pass(reduced, own, other, which, sub):
    outs = []
    wide = widen(sub, 256)
    for quarter in range(4):
        products = dot_nt(reduced, quarter_rows(own, other, which, quarter))
        scores = products * BETA + wide
        peak = jnp.max(scores, axis=0, keepdims=True)
        mass = jnp.sum(jnp.exp2(scores - peak), axis=0, keepdims=True)
        outs.append(peak + log2(mass))
    return lane_to_dense(jnp.concatenate(outs, axis=1))


def swap_halves(values):
    return jnp.concatenate([values[4:8], values[0:4]], axis=0)


def peer_halves(ref, place, offset):
    mine = ref[pl.ds(place * 8, 8), offset : offset + 8, :]
    theirs = ref[pl.ds((1 - place) * 8, 8), offset : offset + 8, :]
    return mine, theirs


def join_sums(ref, place, offset):
    mine, theirs = peer_halves(ref, place, offset)
    return jnp.sum(mine, axis=0) + swap_halves(jnp.sum(theirs, axis=0))


def join_logs(ref, place, offset):
    mine, theirs = peer_halves(ref, place, offset)
    peak = jnp.maximum(jnp.max(mine, axis=0), swap_halves(jnp.max(theirs, axis=0)))
    other_peak = swap_halves(peak)
    mass = jnp.sum(jnp.exp2(mine - peak[None]), axis=0) + swap_halves(
        jnp.sum(jnp.exp2(theirs - other_peak[None]), axis=0)
    )
    return peak + log2(mass)


def lane_index():
    return lax.broadcasted_iota(jnp.int32, (1, 128), 1)


def own_piece(dense, place):
    row = jnp.zeros((1, 128), jnp.float32)
    for k in range(8):
        row = jnp.where(place // 2 == k, dense[k : k + 1, :], row)
    return jnp.where(place % 2 == 0, row, pltpu.roll(row, 64, 1))


def pair_row(first, second):
    return jnp.where(lane_index() < 64, first, pltpu.roll(second, 64, 1))


def piggy_rows(ref, row, place):
    order = []
    for base in (place * 8, (1 - place) * 8):
        for k in range(8):
            order.append(ref[base + k, row : row + 1, :])
    even = jnp.concatenate(order[0::2], axis=0)
    odd = jnp.concatenate(order[1::2], axis=0)
    return even, odd


def unpair(even, odd):
    lane = lax.broadcasted_iota(jnp.int32, (8, 128), 1)
    first = jnp.where(lane < 64, even, pltpu.roll(odd, 64, 1))
    second = jnp.where(lane < 64, pltpu.roll(even, 64, 1), odd)
    return first, second


def canonical_sum(values):
    return jnp.sum(values[0:4], keepdims=True) + jnp.sum(values[4:8], keepdims=True)


def send_all(message_ref, rows):
    message_ref[...] = jnp.broadcast_to(rows[None], message_ref.shape)


def first_half(place, near, across, near_far, across_far, c_own, r_own, r_other, partial):
    side, spot = place[1] // 4, place[1] % 4
    for step in range(4):
        source = lax.rem(spot + 4 - step, 4)
        r_own[pl.ds(side * 4 + source, 1)] = near[step : step + 1]
        r_other[pl.ds(side * 4 + source, 1)] = near_far[step : step + 1]
        r_own[pl.ds((1 - side) * 4 + source, 1)] = across[step : step + 1]
        r_other[pl.ds((1 - side) * 4 + source, 1)] = across_far[step : step + 1]
    y_col = half_rows(c_own, 1)
    partial[...] = peak_pass(y_col, r_own, r_other, 0, -norms_sub(y_col))


def first_rows(r_own, r_other, c_phrases, partial, message):
    y_col = c_phrases[...].reshape(HALF, WIDTH)
    rest = peak_pass(y_col, r_own, r_other, 0, -norms_sub(y_col))
    peak = jnp.maximum(rest, partial[...])
    mass = jnp.exp2(rest - peak) + jnp.exp2(partial[...] - peak)
    send_all(message, peak + log2(mass))


def first_self(r_own, r_other, c_own, c_phrases, c_regions, sums, norms, c_other):
    c_other[:, 0:OWN, :] = c_regions[...]
    c_other[:, OWN : 2 * OWN, :] = c_phrases[...]
    x_row = block_rows(r_own, r_other, 0)
    y_row = block_rows(r_own, r_other, 1)
    x_norm_col = norms_lane(block_rows(c_own, c_other, 0))
    y_norm_col = norms_lane(block_rows(c_own, c_other, 1))
    self_p = sum_pass(x_row, c_own, c_other, 0, -norms_sub(x_row), -x_norm_col)
    self_q = sum_pass(y_row, c_own, c_other, 1, -norms_sub(y_row), -y_norm_col)
    sums[...] = jnp.concatenate([self_p, self_q], axis=0)
    norms[...] = jnp.concatenate(
        [lane_to_dense(v) for v in (norms_lane(x_row), norms_lane(y_row), x_norm_col, y_norm_col)],
        axis=0,
    )


def first_cols(place, r_own, r_other, c_own, c_other, sums, got, message, state):
    u = LOG_COUNT - join_logs(got, place[0], 0)
    x_row = block_rows(r_own, r_other, 0)
    cross = peak_pass(x_row, c_own, c_other, 1, dense_to_sub(u))
    send_all(message, jnp.concatenate([cross, sums[...]], axis=0))
    state[...] = u


def second_rows(place, r_own, r_other, c_own, c_other, norms, state, got, message, h_out):
    spot = place[2]
    h = LOG_COUNT - join_logs(got, place[3], 0)
    p = LOG_COUNT - log2(join_sums(got, place[3], 8))
    q = LOG_COUNT - log2(join_sums(got, place[3], 16))
    x_col = block_rows(c_own, c_other, 0)
    y_col = block_rows(c_own, c_other, 1)
    cross = sum_pass(y_col, r_own, r_other, 0, dense_to_sub(h), dense_to_lane(state[...]))
    self_p = sum_pass(
        x_col, r_own, r_other, 0, dense_to_sub(p - norms[16:24, :]), -dense_to_lane(norms[0:8, :])
    )
    self_q = sum_pass(
        y_col, r_own, r_other, 1, dense_to_sub(q - norms[24:32, :]), -dense_to_lane(norms[8:16, :])
    )
    carry = jnp.broadcast_to(pair_row(own_piece(p, spot), own_piece(q, spot)), (8, 128))
    send_all(message, jnp.concatenate([cross, self_p, self_q, carry], axis=0))
    h_out[...] = h


def second_cols(place, r_own, r_other, c_own, c_other, norms, state, h_in, got, message, shifts):
    core, spot = place[0], place[1]
    p_first, q_first = unpair(*piggy_rows(got, 24, core))
    u = state[...] + (LOG_COUNT - log2(join_sums(got, core, 0)))
    p = 0.5 * (p_first + (LOG_COUNT - log2(join_sums(got, core, 8))))
    q = 0.5 * (q_first + (LOG_COUNT - log2(join_sums(got, core, 16))))
    pt = p - norms[0:8, :]
    qt = q - norms[8:16, :]
    x_row = block_rows(r_own, r_other, 0)
    cross = sum_pass(x_row, c_own, c_other, 1, dense_to_sub(u), dense_to_lane(h_in[...]))
    first = pair_row(own_piece(u, spot), own_piece(pt, spot))
    second = pair_row(own_piece(qt, spot), jnp.zeros((1, 128), jnp.float32))
    total = jnp.broadcast_to(canonical_sum(u - pt - qt), (6, 128))
    send_all(message, jnp.concatenate([cross, first, second, total], axis=0))
    shifts[...] = jnp.concatenate([u, pt, qt], axis=0)


def last_cols(place, h_in, got, message, cols, total):
    h = h_in[...] + (LOG_COUNT - log2(join_sums(got, place[3], 0)))
    u_col, p_col = unpair(*piggy_rows(got, 8, place[3]))
    q_col, unused = unpair(*piggy_rows(got, 9, place[3]))
    piece = own_piece(h, place[2])
    part = jnp.broadcast_to(canonical_sum(h), (7, 128))
    send_all(message, jnp.concatenate([piece, part], axis=0))
    cols[...] = jnp.concatenate([h, u_col, p_col, q_col], axis=0)
    total[...] = jnp.sum(got[:, 8:16, :], axis=0)


def weights(rows, columns, sub, lane):
    products = dot_nt(rows, columns)
    values = jnp.exp2(products * BETA + widen(sub, BLOCK) + lane)
    mass = jnp.sum(values, axis=1, keepdims=True)
    mixed = jnp.dot(values.astype(jnp.bfloat16), columns, preferred_element_type=jnp.float32)
    return mass, mixed


def term(rows, part, columns, sub, lane):
    mass, mixed = weights(rows, columns, sub[part], lane)
    return (rows.astype(jnp.float32) * mass - mixed).reshape(8, OWN, WIDTH)


SECOND = slice(HALF, BLOCK)
FIRST = slice(0, HALF)


def col_lane(cols, k):
    return dense_to_lane(cols[8 * k : 8 * k + 8, :]) - LOG_COUNT


def gradient(rows, part, cross, self_):
    return term(rows, part, *cross) - term(rows, part, *self_)


def region_gradients(r_own, r_other, c_own, c_other, shifts, cols, kept, sent):
    cross = (block_rows(c_own, c_other, 1), dense_to_sub(shifts[0:8, :]), col_lane(cols, 0))
    self_ = (block_rows(c_own, c_other, 0), dense_to_sub(shifts[8:16, :]), col_lane(cols, 2))
    sent[...] = gradient(half_rows(r_other, 0), SECOND, cross, self_)
    kept[...] = gradient(half_rows(r_own, 0), FIRST, cross, self_)


def phrase_gradients(
    place, r_own, r_other, c_own, c_other, shifts, cols, total, got, kept, sent, divergence
):
    h_row, unused = unpair(*piggy_rows(got, 0, place[0]))
    summed = total[...] + jnp.sum(got[...], axis=0)
    divergence[...] = summed * (1.0 / (POINTS * BETA))
    cross = (block_rows(c_own, c_other, 0), dense_to_sub(h_row), col_lane(cols, 1))
    self_ = (block_rows(c_own, c_other, 1), dense_to_sub(shifts[16:24, :]), col_lane(cols, 3))
    sent[...] = gradient(half_rows(r_other, 1), SECOND, cross, self_)
    kept[...] = gradient(half_rows(r_own, 1), FIRST, cross, self_)


def join_gradients(x_kept, x_back, y_kept, y_back, out):
    out[:, 0:OWN, :] = (x_kept[...] + x_back[...]).astype(out.dtype)
    out[:, OWN : 2 * OWN, :] = (y_kept[...] + y_back[...]).astype(out.dtype)


def call(body, outs, smem, passes, *args):
    shapes = [jax.ShapeDtypeStruct(shape, dtype) for shape, dtype in outs]
    specs = [pl.BlockSpec(memory_space=pltpu.VMEM)] * len(args)
    if smem:
        specs[0] = pl.BlockSpec(memory_space=pltpu.SMEM)
    return pl.pallas_call(
        body,
        out_shape=shapes,
        in_specs=specs,
        out_specs=[pl.BlockSpec(memory_space=pltpu.VMEM)] * len(outs),
        compiler_params=pltpu.CompilerParams(vmem_limit_bytes=VMEM_LIMIT),
        cost_estimate=pl.CostEstimate(
            flops=passes * 2 * BLOCK * BLOCK * WIDTH,
            bytes_accessed=4 * BLOCK * WIDTH * 2,
            transcendentals=passes * BLOCK * BLOCK,
        ),
    )(*args)


def share(message, axes, groups=None):
    return lax.all_to_all(message, axes, 0, 0, tiled=True, axis_index_groups=groups)


def share_col(message):
    groups = [
        [far * 16 + z * 2 + (side ^ far) for far in range(2) for z in range(8)] for side in range(2)
    ]
    return share(message, ("xh", "z", "xl"), groups)


def core_swap(values):
    return lax.ppermute(values, "core", [(0, 1), (1, 0)])


def pair_swap(values):
    return lax.ppermute(values, ("xh", "xl"), [(0, 3), (1, 2), (2, 1), (3, 0)])


def y_step(values, shift):
    return lax.ppermute(values, "y", [(y, (y + shift) % 4) for y in range(4)])


def on_device(regions, phrases):
    f32 = jnp.float32
    core = lax.axis_index("core")
    spot_row = lax.axis_index("xl") * 4 + lax.axis_index("y")
    place = jnp.stack([core, spot_row, lax.axis_index("z"), lax.axis_index("xh")]).astype(jnp.int32)

    block = ((8, 2 * OWN, WIDTH), jnp.bfloat16)
    own = jnp.concatenate([regions, phrases], axis=0)
    copies = jnp.broadcast_to(own[None], (8, 2 * OWN, WIDTH))
    copies, own = lax.optimization_barrier((copies, own))
    c_own = share(copies, ("z",))
    c_phrases = pair_swap(c_own[:, OWN : 2 * OWN, :])
    near = jnp.stack([own] + [y_step(own, shift) for shift in (1, 2, 3)])
    across = lax.ppermute(near, "xl", [(0, 1), (1, 0)])
    near_far = core_swap(near)
    across_far = core_swap(across)

    def message(rows):
        return ((16, rows, 128), f32)

    r_own, r_other, partial = call(
        first_half,
        [block, block, ((8, 128), f32)],
        True,
        1,
        place,
        near,
        across,
        near_far,
        across_far,
        c_own,
    )
    partial, c_after = lax.optimization_barrier((partial, c_own))
    c_regions = pair_swap(c_after[:, 0:OWN, :])
    (sent,) = call(first_rows, [message(8)], False, 1, r_own, r_other, c_phrases, partial)
    later, sent = lax.optimization_barrier(((r_own, r_other, c_own, c_phrases), sent))
    got = share(sent, ROW_GROUP)
    sums, norms, c_other = call(
        first_self, [((16, 128), f32), ((32, 128), f32), block], False, 2, *later, c_regions
    )
    points = (r_own, r_other, c_own, c_other)
    sent, state = call(
        first_cols, [message(24), ((8, 128), f32)], True, 1, place, *points, sums, got
    )
    got = share_col(sent)
    sent, h_first = call(
        second_rows, [message(32), ((8, 128), f32)], True, 3, place, *points, norms, state, got
    )
    got = share(sent, ROW_GROUP)
    sent, shifts = call(
        second_cols,
        [message(16), ((24, 128), f32)],
        True,
        1,
        place,
        *points,
        norms,
        state,
        h_first,
        got,
    )
    got = share_col(sent)
    sent, cols, total = call(
        last_cols, [message(8), ((32, 128), f32), ((8, 128), f32)], True, 0, place, h_first, got
    )
    got = share(sent, ROW_GROUP)
    half = ((8, OWN, WIDTH), f32)
    x_kept, x_away = call(region_gradients, [half, half], False, 4, *points, shifts, cols)
    x_back = core_swap(x_away)
    y_kept, y_away, divergence = call(
        phrase_gradients,
        [half, half, ((8, 128), f32)],
        True,
        4,
        place,
        *points,
        shifts,
        cols,
        total,
        got,
    )
    y_back, divergence = lax.optimization_barrier((core_swap(y_away), divergence[2, 0]))
    (joined,) = call(join_gradients, [block], False, 0, x_kept, x_back, y_kept, y_back)
    parts = share(joined, ("xl", "y")).astype(f32)
    summed = jnp.sum(parts, axis=0)
    return (summed[0:OWN], summed[OWN : 2 * OWN], divergence)


def solution(mesh):
    fine = Mesh(mesh.devices.reshape(2, 8, 2, 2, 4), AXES)
    return jax.shard_map(
        on_device,
        mesh=fine,
        in_specs=(P(AXES, None), P(AXES, None)),
        out_specs=(P(AXES, None), P(AXES, None), P()),
        check_vma=False,
    )
```

```python
import math

import jax
import jax.numpy as jnp
from jax import lax
from jax.experimental import pallas as pl
from jax.experimental.pallas import tpu as pltpu
from jax.sharding import Mesh
from jax.sharding import PartitionSpec as P

EPSILON = 0.1
POINTS = 16384
OWN = 64
WIDTH = 256
HALF = 512
BLOCK = 1024
LOG_COUNT = math.log2(POINTS)
BETA = 1.0 / (EPSILON * math.log(2.0))
INV_LN2 = 1.0 / math.log(2.0)

AXES = ("xh", "z", "core", "xl", "y")
ROW_GROUP = ("core", "xl", "y")

VMEM_LIMIT = 20 * 1024 * 1024


def log2(values):
    return jnp.log(values) * INV_LN2


def dot_nt(left, right):
    return lax.dot_general(left, right, (((1,), (1,)), ((), ())), preferred_element_type=jnp.float32)


def dense_to_sub(values):
    pieces = [jnp.broadcast_to(values[t : t + 1, :], (128, 128)).T for t in range(8)]
    return jnp.concatenate(pieces, axis=0)


def dense_to_lane(values):
    return jnp.concatenate([values[t : t + 1, :] for t in range(8)], axis=1)


def lane_to_dense(values):
    return jnp.concatenate([values[:, t * 128 : (t + 1) * 128] for t in range(8)], axis=0)


def widen(sub, lanes):
    return jnp.concatenate([sub] * (lanes // 128), axis=1)


def block_rows(own, other, which):
    parts = [ref[:, which * OWN : (which + 1) * OWN, :].reshape(HALF, WIDTH) for ref in (own, other)]
    return jnp.concatenate(parts, axis=0)


def quarter_rows(own, other, which, quarter):
    ref = own if quarter < 2 else other
    start = (quarter % 2) * 4
    return ref[start : start + 4, which * OWN : (which + 1) * OWN, :].reshape(256, WIDTH)


def half_rows(ref, which):
    return ref[:, which * OWN : (which + 1) * OWN, :].reshape(HALF, WIDTH)


def squares_split(rows):
    values = rows.astype(jnp.float32)
    squares = values * values
    high = squares.astype(jnp.bfloat16)
    low = (squares - high.astype(jnp.float32)).astype(jnp.bfloat16)
    return high, low


def norms_sub(rows):
    high, low = squares_split(rows)
    ones = jnp.ones((WIDTH, 128), jnp.bfloat16)
    total = jnp.dot(high, ones, preferred_element_type=jnp.float32) + jnp.dot(
        low, ones, preferred_element_type=jnp.float32
    )
    return total * (0.5 * BETA)


def norms_lane(rows):
    high, low = squares_split(rows)
    ones = jnp.ones((8, WIDTH), jnp.bfloat16)
    total = dot_nt(ones, high) + dot_nt(ones, low)
    return total[0:1, :] * (0.5 * BETA)


def sum_pass(reduced, own, other, which, sub, lane):
    outs = []
    wide = widen(sub, 256)
    for quarter in range(4):
        products = dot_nt(reduced, quarter_rows(own, other, which, quarter))
        part = lane[:, quarter * 256 : (quarter + 1) * 256]
        outs.append(jnp.sum(jnp.exp2(products * BETA + wide + part), axis=0, keepdims=True))
    return lane_to_dense(jnp.concatenate(outs, axis=1))


def peak_pass(reduced, own, other, which, sub):
    outs = []
    wide = widen(sub, 256)
    for quarter in range(4):
        products = dot_nt(reduced, quarter_rows(own, other, which, quarter))
        scores = products * BETA + wide
        peak = jnp.max(scores, axis=0, keepdims=True)
        mass = jnp.sum(jnp.exp2(scores - peak), axis=0, keepdims=True)
        outs.append(peak + log2(mass))
    return lane_to_dense(jnp.concatenate(outs, axis=1))


def swap_halves(values):
    return jnp.concatenate([values[4:8], values[0:4]], axis=0)


def peer_halves(ref, place, offset):
    mine = ref[pl.ds(place * 8, 8), offset : offset + 8, :]
    theirs = ref[pl.ds((1 - place) * 8, 8), offset : offset + 8, :]
    return mine, theirs


def join_sums(ref, place, offset):
    mine, theirs = peer_halves(ref, place, offset)
    return jnp.sum(mine, axis=0) + swap_halves(jnp.sum(theirs, axis=0))


def join_logs(ref, place, offset):
    mine, theirs = peer_halves(ref, place, offset)
    peak = jnp.maximum(jnp.max(mine, axis=0), swap_halves(jnp.max(theirs, axis=0)))
    other_peak = swap_halves(peak)
    mass = jnp.sum(jnp.exp2(mine - peak[None]), axis=0) + swap_halves(
        jnp.sum(jnp.exp2(theirs - other_peak[None]), axis=0)
    )
    return peak + log2(mass)


def lane_index():
    return lax.broadcasted_iota(jnp.int32, (1, 128), 1)


def own_piece(dense, place):
    row = jnp.zeros((1, 128), jnp.float32)
    for k in range(8):
        row = jnp.where(place // 2 == k, dense[k : k + 1, :], row)
    return jnp.where(place % 2 == 0, row, pltpu.roll(row, 64, 1))


def pair_row(first, second):
    return jnp.where(lane_index() < 64, first, pltpu.roll(second, 64, 1))


def piggy_rows(ref, row, place):
    order = []
    for base in (place * 8, (1 - place) * 8):
        for k in range(8):
            order.append(ref[base + k, row : row + 1, :])
    even = jnp.concatenate(order[0::2], axis=0)
    odd = jnp.concatenate(order[1::2], axis=0)
    return even, odd


def unpair(even, odd):
    lane = lax.broadcasted_iota(jnp.int32, (8, 128), 1)
    first = jnp.where(lane < 64, even, pltpu.roll(odd, 64, 1))
    second = jnp.where(lane < 64, pltpu.roll(even, 64, 1), odd)
    return first, second


def canonical_sum(values):
    return jnp.sum(values[0:4], keepdims=True) + jnp.sum(values[4:8], keepdims=True)


def send_all(message_ref, rows):
    message_ref[...] = jnp.broadcast_to(rows[None], message_ref.shape)


def first_half(near, across, near_far, across_far, c_own, r_own, r_other, partial):
    side, spot = lax.axis_index("xl"), lax.axis_index("y")
    for step in range(4):
        source = lax.rem(spot + 4 - step, 4)
        r_own[pl.ds(side * 4 + source, 1)] = near[step : step + 1]
        r_other[pl.ds(side * 4 + source, 1)] = near_far[step : step + 1]
        r_own[pl.ds((1 - side) * 4 + source, 1)] = across[step : step + 1]
        r_other[pl.ds((1 - side) * 4 + source, 1)] = across_far[step : step + 1]
    y_col = half_rows(c_own, 1)
    partial[...] = peak_pass(y_col, r_own, r_other, 0, -norms_sub(y_col))


def first_rows(r_own, r_other, c_phrases, partial, message):
    y_col = c_phrases[...].reshape(HALF, WIDTH)
    rest = peak_pass(y_col, r_own, r_other, 0, -norms_sub(y_col))
    peak = jnp.maximum(rest, partial[...])
    mass = jnp.exp2(rest - peak) + jnp.exp2(partial[...] - peak)
    send_all(message, peak + log2(mass))


def first_self(r_own, r_other, c_own, c_phrases, c_regions, sums, norms, c_other):
    c_other[:, 0:OWN, :] = c_regions[...]
    c_other[:, OWN : 2 * OWN, :] = c_phrases[...]
    x_row = block_rows(r_own, r_other, 0)
    y_row = block_rows(r_own, r_other, 1)
    x_norm_col = norms_lane(block_rows(c_own, c_other, 0))
    y_norm_col = norms_lane(block_rows(c_own, c_other, 1))
    self_p = sum_pass(x_row, c_own, c_other, 0, -norms_sub(x_row), -x_norm_col)
    self_q = sum_pass(y_row, c_own, c_other, 1, -norms_sub(y_row), -y_norm_col)
    sums[...] = jnp.concatenate([self_p, self_q], axis=0)
    norms[...] = jnp.concatenate(
        [lane_to_dense(v) for v in (norms_lane(x_row), norms_lane(y_row), x_norm_col, y_norm_col)],
        axis=0,
    )


def first_cols(r_own, r_other, c_own, c_other, sums, got, message, state):
    u = LOG_COUNT - join_logs(got, lax.axis_index("core"), 0)
    x_row = block_rows(r_own, r_other, 0)
    cross = peak_pass(x_row, c_own, c_other, 1, dense_to_sub(u))
    send_all(message, jnp.concatenate([cross, sums[...]], axis=0))
    state[...] = u


def second_rows(r_own, r_other, c_own, c_other, norms, state, got, message, h_out):
    far, spot = lax.axis_index("xh"), lax.axis_index("z")
    h = LOG_COUNT - join_logs(got, far, 0)
    p = LOG_COUNT - log2(join_sums(got, far, 8))
    q = LOG_COUNT - log2(join_sums(got, far, 16))
    x_col = block_rows(c_own, c_other, 0)
    y_col = block_rows(c_own, c_other, 1)
    cross = sum_pass(y_col, r_own, r_other, 0, dense_to_sub(h), dense_to_lane(state[...]))
    self_p = sum_pass(
        x_col, r_own, r_other, 0, dense_to_sub(p - norms[16:24, :]), -dense_to_lane(norms[0:8, :])
    )
    self_q = sum_pass(
        y_col, r_own, r_other, 1, dense_to_sub(q - norms[24:32, :]), -dense_to_lane(norms[8:16, :])
    )
    carry = pair_row(own_piece(p, spot), own_piece(q, spot))
    other = jnp.broadcast_to(own_piece(h, spot), (7, 128))
    send_all(message, jnp.concatenate([cross, self_p, self_q, carry, other], axis=0))
    h_out[...] = h


def second_cols(r_own, r_other, c_own, c_other, norms, state, h_in, got, message, shifts):
    core, spot = lax.axis_index("core"), lax.axis_index("xl") * 4 + lax.axis_index("y")
    p_first, q_first = unpair(*piggy_rows(got, 24, core))
    h_row, unused = unpair(*piggy_rows(got, 25, core))
    u = state[...] + (LOG_COUNT - log2(join_sums(got, core, 0)))
    p = 0.5 * (p_first + (LOG_COUNT - log2(join_sums(got, core, 8))))
    q = 0.5 * (q_first + (LOG_COUNT - log2(join_sums(got, core, 16))))
    pt = p - norms[0:8, :]
    qt = q - norms[8:16, :]
    x_row = block_rows(r_own, r_other, 0)
    cross = sum_pass(x_row, c_own, c_other, 1, dense_to_sub(u), dense_to_lane(h_in[...]))
    first = pair_row(own_piece(u, spot), own_piece(pt, spot))
    second = pair_row(own_piece(qt, spot), jnp.zeros((1, 128), jnp.float32))
    total = jnp.broadcast_to(canonical_sum(u - pt - qt), (6, 128))
    send_all(message, jnp.concatenate([cross, first, second, total], axis=0))
    shifts[...] = jnp.concatenate([u, pt, qt, h_row], axis=0)


def weights(rows, columns, sub, lane):
    products = dot_nt(rows, columns)
    values = jnp.exp2(products * BETA + widen(sub, BLOCK) + lane)
    mass = jnp.sum(values, axis=1, keepdims=True)
    mixed = jnp.dot(values.astype(jnp.bfloat16), columns, preferred_element_type=jnp.float32)
    return mass, mixed


def term(rows, part, columns, sub, lane):
    mass, mixed = weights(rows, columns, sub[part], lane)
    return (rows.astype(jnp.float32) * mass - mixed).reshape(8, OWN, WIDTH)


SECOND = slice(HALF, BLOCK)
FIRST = slice(0, HALF)


def gradient(rows, part, cross, self_):
    return term(rows, part, *cross) - term(rows, part, *self_)


def region_gradients(
    r_own, r_other, c_own, c_other, shifts, h_in, got, kept, sent, cols, scale, sums
):
    far = lax.axis_index("xh")
    change = LOG_COUNT - log2(join_sums(got, far, 0))
    h = h_in[...] + change
    u_col, p_col = unpair(*piggy_rows(got, 8, far))
    q_col, unused = unpair(*piggy_rows(got, 9, far))
    cols[...] = jnp.concatenate([u_col, q_col], axis=0) - LOG_COUNT
    own_change = jnp.broadcast_to(own_piece(change, lax.axis_index("z")), (128, 128)).T
    scale[...] = widen(jnp.exp2(own_change[0:OWN, :]), WIDTH)
    total = jnp.sum(got[:, 8:16, :], axis=0)
    part = jnp.broadcast_to(canonical_sum(h), (8, 128))
    sums[...] = jnp.concatenate([jnp.broadcast_to(total[2:3], (8, 128)), part], axis=0)
    h_lane = dense_to_lane(h) - LOG_COUNT
    cross = (block_rows(c_own, c_other, 1), dense_to_sub(shifts[0:8, :]), h_lane)
    p_lane = dense_to_lane(p_col) - LOG_COUNT
    self_ = (block_rows(c_own, c_other, 0), dense_to_sub(shifts[8:16, :]), p_lane)
    sent[...] = gradient(half_rows(r_other, 0), SECOND, cross, self_)
    kept[...] = gradient(half_rows(r_own, 0), FIRST, cross, self_)


def phrase_gradients(
    r_own, r_other, c_own, c_other, shifts, cols, kept, sent, cross_kept, cross_sent
):
    cross = (
        block_rows(c_own, c_other, 0),
        dense_to_sub(shifts[24:32, :]),
        dense_to_lane(cols[0:8, :]),
    )
    self_ = (
        block_rows(c_own, c_other, 1),
        dense_to_sub(shifts[16:24, :]),
        dense_to_lane(cols[8:16, :]),
    )
    for ref, part, out, cross_out in (
        (r_other, SECOND, sent, cross_sent),
        (r_own, FIRST, kept, cross_kept),
    ):
        rows = half_rows(ref, 1)
        cross_out[...] = term(rows, part, *cross)
        out[...] = cross_out[...] - term(rows, part, *self_)


def join_gradients(
    x_kept, x_back, y_kept, y_back, cross_kept, cross_back, sums, sum_back, out
):
    kept_back = ((x_kept, x_back), (y_kept, y_back), (cross_kept, cross_back))
    for k, (kept, back) in enumerate(kept_back):
        out[:, k * OWN : (k + 1) * OWN, :] = (kept[...] + back[...]).astype(out.dtype)
    part = jnp.broadcast_to(sums[8:9, :] + sum_back[8:9, :], (16, 128))
    high = part.astype(jnp.bfloat16)
    left = part - high.astype(jnp.float32)
    middle = left.astype(jnp.bfloat16)
    low = left - middle.astype(jnp.float32)
    row = lax.broadcasted_iota(jnp.int32, (16, 128), 0)
    rest = jnp.where(row < 8, left, low).astype(jnp.bfloat16)
    tail = jnp.concatenate([high, rest], axis=1)
    out[:, 3 * OWN :, :] = jnp.broadcast_to(tail[None], (8, 16, WIDTH))


def finish(parts, scale, sums, grad_x, grad_y, divergence):
    summed = jnp.sum(parts[...].astype(jnp.float32), axis=0)
    grad_x[...] = summed[0:OWN]
    grad_y[...] = summed[OWN : 2 * OWN] + (scale[...] - 1.0) * summed[2 * OWN : 3 * OWN]
    high = summed[192:193, 0:128]
    whole = high + (summed[192:193, 128:256] + summed[200:201, 128:256])
    divergence[...] = (whole + sums[0:1, :])[0:1, 0:1] * (1.0 / (POINTS * BETA))


def call(body, outs, passes, *args):
    shapes = [jax.ShapeDtypeStruct(shape, dtype) for shape, dtype in outs]
    specs = [pl.BlockSpec(memory_space=pltpu.VMEM)] * len(args)
    return pl.pallas_call(
        body,
        out_shape=shapes,
        in_specs=specs,
        out_specs=[pl.BlockSpec(memory_space=pltpu.VMEM)] * len(outs),
        compiler_params=pltpu.CompilerParams(vmem_limit_bytes=VMEM_LIMIT),
        cost_estimate=pl.CostEstimate(
            flops=passes * 2 * BLOCK * BLOCK * WIDTH,
            bytes_accessed=4 * BLOCK * WIDTH * 2,
            transcendentals=passes * BLOCK * BLOCK,
        ),
    )(*args)


def share(message, axes, groups=None):
    return lax.all_to_all(message, axes, 0, 0, tiled=True, axis_index_groups=groups)


def share_col(message):
    groups = [
        [far * 16 + z * 2 + (side ^ far) for far in range(2) for z in range(8)] for side in range(2)
    ]
    return share(message, ("xh", "z", "xl"), groups)


def core_swap(values):
    return lax.ppermute(values, "core", [(0, 1), (1, 0)])


def pair_swap(values):
    return lax.ppermute(values, ("xh", "xl"), [(0, 3), (1, 2), (2, 1), (3, 0)])


def y_step(values, shift):
    return lax.ppermute(values, "y", [(y, (y + shift) % 4) for y in range(4)])


def on_device(regions, phrases):
    f32 = jnp.float32
    block = ((8, 2 * OWN, WIDTH), jnp.bfloat16)
    spread = [jnp.broadcast_to(points[None], (8, OWN, WIDTH)) for points in (regions, phrases)]
    copies, regions, phrases = lax.optimization_barrier(
        (jnp.concatenate(spread, axis=1), regions, phrases)
    )
    own = jnp.concatenate([regions, phrases], axis=0)
    c_own = share(copies, ("z",))
    c_phrases = pair_swap(c_own[:, OWN : 2 * OWN, :])
    near = jnp.stack([own] + [y_step(own, shift) for shift in (1, 2, 3)])
    across = lax.ppermute(near, "xl", [(0, 1), (1, 0)])
    near_far = core_swap(near)
    across_far = core_swap(across)

    def message(rows):
        return ((16, rows, 128), f32)

    r_own, r_other, partial = call(
        first_half,
        [block, block, ((8, 128), f32)],
        1,
        near,
        across,
        near_far,
        across_far,
        c_own,
    )
    partial, c_after = lax.optimization_barrier((partial, c_own))
    c_regions = pair_swap(c_after[:, 0:OWN, :])
    (sent,) = call(first_rows, [message(8)], 1, r_own, r_other, c_phrases, partial)
    later, sent = lax.optimization_barrier(((r_own, r_other, c_own, c_phrases), sent))
    got = share(sent, ROW_GROUP)
    sums, norms, c_other = call(
        first_self, [((16, 128), f32), ((32, 128), f32), block], 2, *later, c_regions
    )
    points = (r_own, r_other, c_own, c_other)
    sent, state = call(
        first_cols, [message(24), ((8, 128), f32)], 1, *points, sums, got
    )
    got = share_col(sent)
    sent, h_first = call(
        second_rows, [message(32), ((8, 128), f32)], 3, *points, norms, state, got
    )
    got = share(sent, ROW_GROUP)
    sent, shifts = call(
        second_cols,
        [message(16), ((32, 128), f32)],
        1,
        *points,
        norms,
        state,
        h_first,
        got,
    )
    got = share_col(sent)
    half = ((8, OWN, WIDTH), f32)
    x_kept, x_away, cols, scale, sums = call(
        region_gradients,
        [half, half, ((16, 128), f32), ((OWN, WIDTH), f32), ((16, 128), f32)],
        2,
        *points,
        shifts,
        h_first,
        got,
    )
    x_back, sum_back = core_swap(x_away), core_swap(sums)
    y_kept, y_away, cross_kept, cross_away = call(
        phrase_gradients, [half] * 4, 2, *points, shifts, cols
    )
    y_back, cross_back = core_swap(y_away), core_swap(cross_away)
    (joined,) = call(
        join_gradients,
        [((8, 3 * OWN + 16, WIDTH), jnp.bfloat16)],
        0,
        x_kept,
        x_back,
        y_kept,
        y_back,
        cross_kept,
        cross_back,
        sums,
        sum_back,
    )
    grad_x, grad_y, divergence = call(
        finish,
        [((OWN, WIDTH), f32), ((OWN, WIDTH), f32), ((1, 1), f32)],
        0,
        share(joined, ("xl", "y")),
        scale,
        sums,
    )
    return (grad_x, grad_y, divergence[0, 0])


def solution(mesh):
    fine = Mesh(mesh.devices.reshape(2, 8, 2, 2, 4), AXES)
    return jax.shard_map(
        on_device,
        mesh=fine,
        in_specs=(P(AXES, None), P(AXES, None)),
        out_specs=(P(AXES, None), P(AXES, None), P()),
        check_vma=False,
    )
```

```python
import math

import jax
import jax.numpy as jnp
from jax import lax
from jax.experimental import pallas as pl
from jax.experimental.pallas import tpu as pltpu
from jax.sharding import Mesh
from jax.sharding import PartitionSpec as P

EPSILON = 0.1
POINTS = 16384
OWN = 64
WIDTH = 256
HALF = 512
BLOCK = 1024
LOG_COUNT = math.log2(POINTS)
BETA = 1.0 / (EPSILON * math.log(2.0))
INV_LN2 = 1.0 / math.log(2.0)

AXES = ("xh", "z", "core", "xl", "y")
ROW_GROUP = ("core", "xl", "y")

VMEM_LIMIT = 20 * 1024 * 1024


def log2(values):
    return jnp.log(values) * INV_LN2


def dot_nt(left, right):
    return lax.dot_general(left, right, (((1,), (1,)), ((), ())), preferred_element_type=jnp.float32)


def dense_to_sub(values):
    pieces = [jnp.broadcast_to(values[t : t + 1, :], (128, 128)).T for t in range(8)]
    return jnp.concatenate(pieces, axis=0)


def dense_to_lane(values):
    return jnp.concatenate([values[t : t + 1, :] for t in range(8)], axis=1)


def lane_to_dense(values):
    return jnp.concatenate([values[:, t * 128 : (t + 1) * 128] for t in range(8)], axis=0)


def widen(sub, lanes):
    return jnp.concatenate([sub] * (lanes // 128), axis=1)


def block_rows(own, other, which):
    parts = [ref[:, which * OWN : (which + 1) * OWN, :].reshape(HALF, WIDTH) for ref in (own, other)]
    return jnp.concatenate(parts, axis=0)


def quarter_rows(own, other, which, quarter):
    ref = own if quarter < 2 else other
    start = (quarter % 2) * 4
    return ref[start : start + 4, which * OWN : (which + 1) * OWN, :].reshape(256, WIDTH)


def half_rows(ref, which):
    return ref[:, which * OWN : (which + 1) * OWN, :].reshape(HALF, WIDTH)


def squares_split(rows):
    values = rows.astype(jnp.float32)
    squares = values * values
    high = squares.astype(jnp.bfloat16)
    low = (squares - high.astype(jnp.float32)).astype(jnp.bfloat16)
    return high, low


def norms_sub(rows):
    high, low = squares_split(rows)
    ones = jnp.ones((WIDTH, 128), jnp.bfloat16)
    total = jnp.dot(high, ones, preferred_element_type=jnp.float32) + jnp.dot(
        low, ones, preferred_element_type=jnp.float32
    )
    return total * (0.5 * BETA)


def norms_lane(rows):
    high, low = squares_split(rows)
    ones = jnp.ones((8, WIDTH), jnp.bfloat16)
    total = dot_nt(ones, high) + dot_nt(ones, low)
    return total[0:1, :] * (0.5 * BETA)


def sum_pass(reduced, own, other, which, sub, lane):
    outs = []
    wide = widen(sub, 256)
    for quarter in range(4):
        products = dot_nt(reduced, quarter_rows(own, other, which, quarter))
        part = lane[:, quarter * 256 : (quarter + 1) * 256]
        outs.append(jnp.sum(jnp.exp2(products * BETA + wide + part), axis=0, keepdims=True))
    return lane_to_dense(jnp.concatenate(outs, axis=1))


def peak_pass(reduced, own, other, which, sub):
    outs = []
    wide = widen(sub, 256)
    for quarter in range(4):
        products = dot_nt(reduced, quarter_rows(own, other, which, quarter))
        scores = products * BETA + wide
        peak = jnp.max(scores, axis=0, keepdims=True)
        mass = jnp.sum(jnp.exp2(scores - peak), axis=0, keepdims=True)
        outs.append(peak + log2(mass))
    return lane_to_dense(jnp.concatenate(outs, axis=1))


def swap_halves(values):
    return jnp.concatenate([values[4:8], values[0:4]], axis=0)


def peer_halves(ref, place, offset):
    mine = ref[pl.ds(place * 8, 8), offset : offset + 8, :]
    theirs = ref[pl.ds((1 - place) * 8, 8), offset : offset + 8, :]
    return mine, theirs


def join_sums(ref, place, offset):
    mine, theirs = peer_halves(ref, place, offset)
    return jnp.sum(mine, axis=0) + swap_halves(jnp.sum(theirs, axis=0))


def join_logs(ref, place, offset):
    mine, theirs = peer_halves(ref, place, offset)
    peak = jnp.maximum(jnp.max(mine, axis=0), swap_halves(jnp.max(theirs, axis=0)))
    other_peak = swap_halves(peak)
    mass = jnp.sum(jnp.exp2(mine - peak[None]), axis=0) + swap_halves(
        jnp.sum(jnp.exp2(theirs - other_peak[None]), axis=0)
    )
    return peak + log2(mass)


def lane_index():
    return lax.broadcasted_iota(jnp.int32, (1, 128), 1)


def own_piece(dense, place):
    row = jnp.zeros((1, 128), jnp.float32)
    for k in range(8):
        row = jnp.where(place // 2 == k, dense[k : k + 1, :], row)
    return jnp.where(place % 2 == 0, row, pltpu.roll(row, 64, 1))


def pair_row(first, second):
    return jnp.where(lane_index() < 64, first, pltpu.roll(second, 64, 1))


def piggy_rows(ref, row, place):
    order = []
    for base in (place * 8, (1 - place) * 8):
        for k in range(8):
            order.append(ref[base + k, row : row + 1, :])
    even = jnp.concatenate(order[0::2], axis=0)
    odd = jnp.concatenate(order[1::2], axis=0)
    return even, odd


def unpair(even, odd):
    lane = lax.broadcasted_iota(jnp.int32, (8, 128), 1)
    first = jnp.where(lane < 64, even, pltpu.roll(odd, 64, 1))
    second = jnp.where(lane < 64, pltpu.roll(even, 64, 1), odd)
    return first, second


def canonical_sum(values):
    return jnp.sum(values[0:4], keepdims=True) + jnp.sum(values[4:8], keepdims=True)


def send_all(message_ref, rows):
    message_ref[...] = jnp.broadcast_to(rows[None], message_ref.shape)


def spread(own, paired, copies):
    copies[:, 0 : 2 * OWN, :] = jnp.broadcast_to(own[...][None], (8, 2 * OWN, WIDTH))
    copies[:, 2 * OWN :, :] = jnp.broadcast_to(paired[...][None], (8, OWN, WIDTH))


def first_rows(near, across, near_far, across_far, c_own, message, r_own, r_other):
    side, spot = lax.axis_index("xl"), lax.axis_index("y")
    for step in range(4):
        source = lax.rem(spot + 4 - step, 4)
        r_own[pl.ds(side * 4 + source, 1)] = near[step : step + 1]
        r_other[pl.ds(side * 4 + source, 1)] = near_far[step : step + 1]
        r_own[pl.ds((1 - side) * 4 + source, 1)] = across[step : step + 1]
        r_other[pl.ds((1 - side) * 4 + source, 1)] = across_far[step : step + 1]
    y_col = jnp.concatenate([half_rows(c_own, 1), half_rows(c_own, 2)], axis=0)
    send_all(message, peak_pass(y_col, r_own, r_other, 0, -norms_sub(y_col)))


def first_self(r_own, r_other, c_own, c_regions, sums, norms, c_other):
    c_other[:, 0:OWN, :] = c_regions[...]
    c_other[:, OWN : 2 * OWN, :] = c_own[:, 2 * OWN : 3 * OWN, :]
    x_row = block_rows(r_own, r_other, 0)
    y_row = block_rows(r_own, r_other, 1)
    x_norm_col = norms_lane(block_rows(c_own, c_other, 0))
    y_norm_col = norms_lane(block_rows(c_own, c_other, 1))
    self_p = sum_pass(x_row, c_own, c_other, 0, -norms_sub(x_row), -x_norm_col)
    self_q = sum_pass(y_row, c_own, c_other, 1, -norms_sub(y_row), -y_norm_col)
    sums[...] = jnp.concatenate([self_p, self_q], axis=0)
    norms[...] = jnp.concatenate(
        [lane_to_dense(v) for v in (norms_lane(x_row), norms_lane(y_row), x_norm_col, y_norm_col)],
        axis=0,
    )


def first_cols(r_own, r_other, c_own, c_other, sums, got, message, state):
    u = LOG_COUNT - join_logs(got, lax.axis_index("core"), 0)
    x_row = block_rows(r_own, r_other, 0)
    cross = peak_pass(x_row, c_own, c_other, 1, dense_to_sub(u))
    send_all(message, jnp.concatenate([cross, sums[...]], axis=0))
    state[...] = u


def second_rows(r_own, r_other, c_own, c_other, norms, state, got, message, h_out):
    far, spot = lax.axis_index("xh"), lax.axis_index("z")
    h = LOG_COUNT - join_logs(got, far, 0)
    p = LOG_COUNT - log2(join_sums(got, far, 8))
    q = LOG_COUNT - log2(join_sums(got, far, 16))
    x_col = block_rows(c_own, c_other, 0)
    y_col = block_rows(c_own, c_other, 1)
    cross = sum_pass(y_col, r_own, r_other, 0, dense_to_sub(h), dense_to_lane(state[...]))
    self_p = sum_pass(
        x_col, r_own, r_other, 0, dense_to_sub(p - norms[16:24, :]), -dense_to_lane(norms[0:8, :])
    )
    self_q = sum_pass(
        y_col, r_own, r_other, 1, dense_to_sub(q - norms[24:32, :]), -dense_to_lane(norms[8:16, :])
    )
    carry = pair_row(own_piece(p, spot), own_piece(q, spot))
    other = jnp.broadcast_to(own_piece(h, spot), (7, 128))
    send_all(message, jnp.concatenate([cross, self_p, self_q, carry, other], axis=0))
    h_out[...] = h


def second_cols(r_own, r_other, c_own, c_other, norms, state, h_in, got, message, shifts):
    core, spot = lax.axis_index("core"), lax.axis_index("xl") * 4 + lax.axis_index("y")
    p_first, q_first = unpair(*piggy_rows(got, 24, core))
    h_row, unused = unpair(*piggy_rows(got, 25, core))
    u = state[...] + (LOG_COUNT - log2(join_sums(got, core, 0)))
    p = 0.5 * (p_first + (LOG_COUNT - log2(join_sums(got, core, 8))))
    q = 0.5 * (q_first + (LOG_COUNT - log2(join_sums(got, core, 16))))
    pt = p - norms[0:8, :]
    qt = q - norms[8:16, :]
    x_row = block_rows(r_own, r_other, 0)
    cross = sum_pass(x_row, c_own, c_other, 1, dense_to_sub(u), dense_to_lane(h_in[...]))
    first = pair_row(own_piece(u, spot), own_piece(pt, spot))
    second = pair_row(own_piece(qt, spot), jnp.zeros((1, 128), jnp.float32))
    total = jnp.broadcast_to(canonical_sum(u - pt - qt), (6, 128))
    send_all(message, jnp.concatenate([cross, first, second, total], axis=0))
    shifts[...] = jnp.concatenate([u, pt, qt, h_row], axis=0)


def weights(rows, columns, sub, lane):
    products = dot_nt(rows, columns)
    values = jnp.exp2(products * BETA + widen(sub, BLOCK) + lane)
    mass = jnp.sum(values, axis=1, keepdims=True)
    mixed = jnp.dot(values.astype(jnp.bfloat16), columns, preferred_element_type=jnp.float32)
    return mass, mixed


def term(rows, part, columns, sub, lane):
    mass, mixed = weights(rows, columns, sub[part], lane)
    return (rows.astype(jnp.float32) * mass - mixed).reshape(8, OWN, WIDTH)


SECOND = slice(HALF, BLOCK)
FIRST = slice(0, HALF)


def gradient(rows, part, cross, self_):
    return term(rows, part, *cross) - term(rows, part, *self_)


def half_gradients(ref, part, c_own, c_other, shifts, cols, out):
    x_col = block_rows(c_own, c_other, 0)
    y_col = block_rows(c_own, c_other, 1)
    u_sub, p_sub, q_sub, h_sub = [
        dense_to_sub(shifts[8 * k : 8 * k + 8, :]) for k in range(4)
    ]
    h_lane, u_lane, p_lane, q_lane = [
        dense_to_lane(cols[8 * k : 8 * k + 8, :]) - LOG_COUNT for k in range(4)
    ]
    rows = half_rows(ref, 0)
    out[:, 0:OWN, :] = gradient(rows, part, (y_col, u_sub, h_lane), (x_col, p_sub, p_lane))
    rows = half_rows(ref, 1)
    cross = term(rows, part, x_col, h_sub, u_lane)
    out[:, 2 * OWN : 3 * OWN, :] = cross
    out[:, OWN : 2 * OWN, :] = cross - term(rows, part, y_col, q_sub, q_lane)


def other_gradients(r_other, c_own, c_other, shifts, h_in, got, sent, cols, scale, sums):
    far = lax.axis_index("xh")
    change = LOG_COUNT - log2(join_sums(got, far, 0))
    h = h_in[...] + change
    u_col, p_col = unpair(*piggy_rows(got, 8, far))
    q_col, unused = unpair(*piggy_rows(got, 9, far))
    cols[...] = jnp.concatenate([h, u_col, p_col, q_col], axis=0)
    own_change = jnp.broadcast_to(own_piece(change, lax.axis_index("z")), (128, 128)).T
    scale[...] = widen(jnp.exp2(own_change[0:OWN, :]), WIDTH)
    total = jnp.sum(got[:, 8:16, :], axis=0)
    part = jnp.broadcast_to(canonical_sum(h), (8, 128))
    sums[...] = jnp.concatenate([jnp.broadcast_to(total[2:3], (8, 128)), part], axis=0)
    half_gradients(r_other, SECOND, c_own, c_other, shifts, cols, sent)


def own_gradients(r_own, c_own, c_other, shifts, cols, kept):
    half_gradients(r_own, FIRST, c_own, c_other, shifts, cols, kept)


def join_gradients(kept, back, sums, sum_back, out):
    out[:, 0 : 3 * OWN, :] = (kept[...] + back[...]).astype(out.dtype)
    part = jnp.broadcast_to(sums[8:9, :] + sum_back[8:9, :], (16, 128))
    high = part.astype(jnp.bfloat16)
    left = part - high.astype(jnp.float32)
    middle = left.astype(jnp.bfloat16)
    low = left - middle.astype(jnp.float32)
    row = lax.broadcasted_iota(jnp.int32, (16, 128), 0)
    rest = jnp.where(row < 8, left, low).astype(jnp.bfloat16)
    tail = jnp.concatenate([high, rest], axis=1)
    out[:, 3 * OWN :, :] = jnp.broadcast_to(tail[None], (8, 16, WIDTH))


def finish(parts, scale, sums, grad_x, grad_y, divergence):
    summed = jnp.sum(parts[...].astype(jnp.float32), axis=0)
    grad_x[...] = summed[0:OWN]
    grad_y[...] = summed[OWN : 2 * OWN] + (scale[...] - 1.0) * summed[2 * OWN : 3 * OWN]
    high = summed[192:193, 0:128]
    whole = high + (summed[192:193, 128:256] + summed[200:201, 128:256])
    divergence[...] = (whole + sums[0:1, :])[0:1, 0:1] * (1.0 / (POINTS * BETA))


def call(body, outs, passes, *args):
    shapes = [jax.ShapeDtypeStruct(shape, dtype) for shape, dtype in outs]
    specs = [pl.BlockSpec(memory_space=pltpu.VMEM)] * len(args)
    return pl.pallas_call(
        body,
        out_shape=shapes,
        in_specs=specs,
        out_specs=[pl.BlockSpec(memory_space=pltpu.VMEM)] * len(outs),
        compiler_params=pltpu.CompilerParams(vmem_limit_bytes=VMEM_LIMIT),
        cost_estimate=pl.CostEstimate(
            flops=passes * 2 * BLOCK * BLOCK * WIDTH,
            bytes_accessed=4 * BLOCK * WIDTH * 2,
            transcendentals=passes * BLOCK * BLOCK,
        ),
    )(*args)


def share(message, axes, groups=None):
    return lax.all_to_all(message, axes, 0, 0, tiled=True, axis_index_groups=groups)


def share_col(message):
    groups = [
        [far * 16 + z * 2 + (side ^ far) for far in range(2) for z in range(8)] for side in range(2)
    ]
    return share(message, ("xh", "z", "xl"), groups)


def core_swap(values):
    return lax.ppermute(values, "core", [(0, 1), (1, 0)])


def pair_swap(values):
    return lax.ppermute(values, ("xh", "xl"), [(0, 3), (1, 2), (2, 1), (3, 0)])


def y_step(values, shift):
    return lax.ppermute(values, "y", [(y, (y + shift) % 4) for y in range(4)])


def on_device(regions, phrases):
    f32 = jnp.float32
    block = ((8, 2 * OWN, WIDTH), jnp.bfloat16)
    own = jnp.concatenate([regions, phrases], axis=0)
    (copies,) = call(
        spread, [((8, 3 * OWN, WIDTH), jnp.bfloat16)], 0, own, pair_swap(phrases)
    )
    c_own = share(copies, ("z",))
    near = jnp.stack([own] + [y_step(own, shift) for shift in (1, 2, 3)])
    across = lax.ppermute(near, "xl", [(0, 1), (1, 0)])
    near_far = core_swap(near)
    across_far = core_swap(across)

    def message(rows):
        return ((16, rows, 128), f32)

    sent, r_own, r_other = call(
        first_rows, [message(8), block, block], 1, near, across, near_far, across_far, c_own
    )
    c_regions = pair_swap(c_own[:, 0:OWN, :])
    later, sent = lax.optimization_barrier(((r_own, r_other, c_own), sent))
    got = share(sent, ROW_GROUP)
    sums, norms, c_other = call(
        first_self, [((16, 128), f32), ((32, 128), f32), block], 2, *later, c_regions
    )
    points = (r_own, r_other, c_own, c_other)
    sent, state = call(
        first_cols, [message(24), ((8, 128), f32)], 1, *points, sums, got
    )
    got = share_col(sent)
    sent, h_first = call(
        second_rows, [message(32), ((8, 128), f32)], 3, *points, norms, state, got
    )
    got = share(sent, ROW_GROUP)
    sent, shifts = call(
        second_cols,
        [message(16), ((32, 128), f32)],
        1,
        *points,
        norms,
        state,
        h_first,
        got,
    )
    got = share_col(sent)
    half = ((8, 3 * OWN, WIDTH), f32)
    away, cols, scale, sums = call(
        other_gradients,
        [half, ((32, 128), f32), ((OWN, WIDTH), f32), ((16, 128), f32)],
        2,
        *points[1:],
        shifts,
        h_first,
        got,
    )
    back, sum_back = core_swap(away), core_swap(sums)
    (kept,) = call(own_gradients, [half], 2, r_own, c_own, c_other, shifts, cols)
    (joined,) = call(
        join_gradients,
        [((8, 3 * OWN + 16, WIDTH), jnp.bfloat16)],
        0,
        kept,
        back,
        sums,
        sum_back,
    )
    grad_x, grad_y, divergence = call(
        finish,
        [((OWN, WIDTH), f32), ((OWN, WIDTH), f32), ((1, 1), f32)],
        0,
        share(joined, ("xl", "y")),
        scale,
        sums,
    )
    return (grad_x, grad_y, divergence[0, 0])


def solution(mesh):
    fine = Mesh(mesh.devices.reshape(2, 8, 2, 2, 4), AXES)
    return jax.shard_map(
        on_device,
        mesh=fine,
        in_specs=(P(AXES, None), P(AXES, None)),
        out_specs=(P(AXES, None), P(AXES, None), P()),
        check_vma=False,
    )
```

```python
import math

import jax
import jax.numpy as jnp
from jax import lax
from jax.experimental import pallas as pl
from jax.experimental.pallas import tpu as pltpu
from jax.sharding import Mesh
from jax.sharding import PartitionSpec as P

EPSILON = 0.1
POINTS = 16384
OWN = 64
WIDTH = 256
HALF = 512
BLOCK = 1024
LOG_COUNT = math.log2(POINTS)
BETA = 1.0 / (EPSILON * math.log(2.0))
INV_LN2 = 1.0 / math.log(2.0)

AXES = ("xh", "z", "core", "xl", "y")
ROW_GROUP = ("core", "xl", "y")

VMEM_LIMIT = 20 * 1024 * 1024


def log2(values):
    return jnp.log(values) * INV_LN2


def dot_nt(left, right):
    return lax.dot_general(left, right, (((1,), (1,)), ((), ())), preferred_element_type=jnp.float32)


def dense_to_sub(values):
    pieces = [jnp.broadcast_to(values[t : t + 1, :], (128, 128)).T for t in range(8)]
    return jnp.concatenate(pieces, axis=0)


def dense_to_lane(values):
    return jnp.concatenate([values[t : t + 1, :] for t in range(8)], axis=1)


def lane_to_dense(values):
    return jnp.concatenate([values[:, t * 128 : (t + 1) * 128] for t in range(8)], axis=0)


def widen(sub, lanes):
    return jnp.concatenate([sub] * (lanes // 128), axis=1)


def block_rows(own, other, which):
    parts = [ref[:, which * OWN : (which + 1) * OWN, :].reshape(HALF, WIDTH) for ref in (own, other)]
    return jnp.concatenate(parts, axis=0)


def quarter_rows(own, other, which, quarter):
    ref = own if quarter < 2 else other
    start = (quarter % 2) * 4
    return ref[start : start + 4, which * OWN : (which + 1) * OWN, :].reshape(256, WIDTH)


def half_rows(ref, which):
    return ref[:, which * OWN : (which + 1) * OWN, :].reshape(HALF, WIDTH)


def squares_split(rows):
    values = rows.astype(jnp.float32)
    squares = values * values
    high = squares.astype(jnp.bfloat16)
    low = (squares - high.astype(jnp.float32)).astype(jnp.bfloat16)
    return high, low


def norms_sub(rows):
    high, low = squares_split(rows)
    ones = jnp.ones((WIDTH, 128), jnp.bfloat16)
    total = jnp.dot(high, ones, preferred_element_type=jnp.float32) + jnp.dot(
        low, ones, preferred_element_type=jnp.float32
    )
    return total * (0.5 * BETA)


def norms_lane(rows):
    high, low = squares_split(rows)
    ones = jnp.ones((8, WIDTH), jnp.bfloat16)
    total = dot_nt(ones, high) + dot_nt(ones, low)
    return total[0:1, :] * (0.5 * BETA)


def sum_pass(reduced, own, other, which, sub, lane):
    outs = []
    wide = widen(sub, 256)
    for quarter in range(4):
        products = dot_nt(reduced, quarter_rows(own, other, which, quarter))
        part = lane[:, quarter * 256 : (quarter + 1) * 256]
        outs.append(jnp.sum(jnp.exp2(products * BETA + wide + part), axis=0, keepdims=True))
    return lane_to_dense(jnp.concatenate(outs, axis=1))


def peak_pass(reduced, own, other, which, sub):
    outs = []
    wide = widen(sub, 256)
    for quarter in range(4):
        products = dot_nt(reduced, quarter_rows(own, other, which, quarter))
        scores = products * BETA + wide
        peak = jnp.max(scores, axis=0, keepdims=True)
        mass = jnp.sum(jnp.exp2(scores - peak), axis=0, keepdims=True)
        outs.append(peak + log2(mass))
    return lane_to_dense(jnp.concatenate(outs, axis=1))


def swap_halves(values):
    return jnp.concatenate([values[4:8], values[0:4]], axis=0)


def peer_halves(ref, place, offset):
    mine = ref[pl.ds(place * 8, 8), offset : offset + 8, :]
    theirs = ref[pl.ds((1 - place) * 8, 8), offset : offset + 8, :]
    return mine, theirs


def join_sums(ref, place, offset):
    mine, theirs = peer_halves(ref, place, offset)
    return jnp.sum(mine, axis=0) + swap_halves(jnp.sum(theirs, axis=0))


def join_logs(ref, place, offset):
    mine, theirs = peer_halves(ref, place, offset)
    peak = jnp.maximum(jnp.max(mine, axis=0), swap_halves(jnp.max(theirs, axis=0)))
    other_peak = swap_halves(peak)
    mass = jnp.sum(jnp.exp2(mine - peak[None]), axis=0) + swap_halves(
        jnp.sum(jnp.exp2(theirs - other_peak[None]), axis=0)
    )
    return peak + log2(mass)


def lane_index():
    return lax.broadcasted_iota(jnp.int32, (1, 128), 1)


def own_piece(dense, place):
    row = jnp.zeros((1, 128), jnp.float32)
    for k in range(8):
        row = jnp.where(place // 2 == k, dense[k : k + 1, :], row)
    return jnp.where(place % 2 == 0, row, pltpu.roll(row, 64, 1))


def pair_row(first, second):
    return jnp.where(lane_index() < 64, first, pltpu.roll(second, 64, 1))


def piggy_rows(ref, row, place):
    order = []
    for base in (place * 8, (1 - place) * 8):
        for k in range(8):
            order.append(ref[base + k, row : row + 1, :])
    even = jnp.concatenate(order[0::2], axis=0)
    odd = jnp.concatenate(order[1::2], axis=0)
    return even, odd


def unpair(even, odd):
    lane = lax.broadcasted_iota(jnp.int32, (8, 128), 1)
    first = jnp.where(lane < 64, even, pltpu.roll(odd, 64, 1))
    second = jnp.where(lane < 64, pltpu.roll(even, 64, 1), odd)
    return first, second


def canonical_sum(values):
    return jnp.sum(values[0:4], keepdims=True) + jnp.sum(values[4:8], keepdims=True)


def send_all(message_ref, rows):
    message_ref[...] = jnp.broadcast_to(rows[None], message_ref.shape)


def spread(own, paired, copies):
    copies[:, 0 : 2 * OWN, :] = jnp.broadcast_to(own[...][None], (8, 2 * OWN, WIDTH))
    copies[:, 2 * OWN :, :] = jnp.broadcast_to(paired[...][None], (8, OWN, WIDTH))


def first_rows(near, across, near_far, across_far, c_own, message, r_own, r_other):
    side, spot = lax.axis_index("xl"), lax.axis_index("y")
    for step in range(4):
        source = lax.rem(spot + 4 - step, 4)
        r_own[pl.ds(side * 4 + source, 1)] = near[step : step + 1]
        r_other[pl.ds(side * 4 + source, 1)] = near_far[step : step + 1]
        r_own[pl.ds((1 - side) * 4 + source, 1)] = across[step : step + 1]
        r_other[pl.ds((1 - side) * 4 + source, 1)] = across_far[step : step + 1]
    y_col = jnp.concatenate([half_rows(c_own, 1), half_rows(c_own, 2)], axis=0)
    send_all(message, peak_pass(y_col, r_own, r_other, 0, -norms_sub(y_col)))


def first_self(r_own, r_other, c_own, c_regions, sums, norms, c_other):
    c_other[:, 0:OWN, :] = c_regions[...]
    c_other[:, OWN : 2 * OWN, :] = c_own[:, 2 * OWN : 3 * OWN, :]
    x_row = block_rows(r_own, r_other, 0)
    y_row = block_rows(r_own, r_other, 1)
    x_norm_col = norms_lane(block_rows(c_own, c_other, 0))
    y_norm_col = norms_lane(block_rows(c_own, c_other, 1))
    self_p = sum_pass(x_row, c_own, c_other, 0, -norms_sub(x_row), -x_norm_col)
    self_q = sum_pass(y_row, c_own, c_other, 1, -norms_sub(y_row), -y_norm_col)
    sums[...] = jnp.concatenate([self_p, self_q], axis=0)
    norms[...] = jnp.concatenate(
        [lane_to_dense(v) for v in (norms_lane(x_row), norms_lane(y_row), x_norm_col, y_norm_col)],
        axis=0,
    )


def first_cols(r_own, r_other, c_own, c_other, sums, got, message, state):
    u = LOG_COUNT - join_logs(got, lax.axis_index("core"), 0)
    x_row = block_rows(r_own, r_other, 0)
    cross = peak_pass(x_row, c_own, c_other, 1, dense_to_sub(u))
    send_all(message, jnp.concatenate([cross, sums[...]], axis=0))
    state[...] = u


def second_rows(r_own, r_other, c_own, c_other, norms, state, got, message, h_out):
    far, spot = lax.axis_index("xh"), lax.axis_index("z")
    h = LOG_COUNT - join_logs(got, far, 0)
    p = LOG_COUNT - log2(join_sums(got, far, 8))
    q = LOG_COUNT - log2(join_sums(got, far, 16))
    x_col = block_rows(c_own, c_other, 0)
    y_col = block_rows(c_own, c_other, 1)
    cross = sum_pass(y_col, r_own, r_other, 0, dense_to_sub(h), dense_to_lane(state[...]))
    self_p = sum_pass(
        x_col, r_own, r_other, 0, dense_to_sub(p - norms[16:24, :]), -dense_to_lane(norms[0:8, :])
    )
    self_q = sum_pass(
        y_col, r_own, r_other, 1, dense_to_sub(q - norms[24:32, :]), -dense_to_lane(norms[8:16, :])
    )
    carry = pair_row(own_piece(p, spot), own_piece(q, spot))
    other = jnp.broadcast_to(own_piece(h, spot), (7, 128))
    send_all(message, jnp.concatenate([cross, self_p, self_q, carry, other], axis=0))
    h_out[...] = h


def second_cols(r_own, r_other, c_own, c_other, norms, state, h_in, got, message, shifts):
    core, spot = lax.axis_index("core"), lax.axis_index("xl") * 4 + lax.axis_index("y")
    p_first, q_first = unpair(*piggy_rows(got, 24, core))
    h_row, unused = unpair(*piggy_rows(got, 25, core))
    u = state[...] + (LOG_COUNT - log2(join_sums(got, core, 0)))
    p = 0.5 * (p_first + (LOG_COUNT - log2(join_sums(got, core, 8))))
    q = 0.5 * (q_first + (LOG_COUNT - log2(join_sums(got, core, 16))))
    pt = p - norms[0:8, :]
    qt = q - norms[8:16, :]
    x_row = block_rows(r_own, r_other, 0)
    cross = sum_pass(x_row, c_own, c_other, 1, dense_to_sub(u), dense_to_lane(h_in[...]))
    first = pair_row(own_piece(u, spot), own_piece(pt, spot))
    second = pair_row(own_piece(qt, spot), jnp.zeros((1, 128), jnp.float32))
    total = jnp.broadcast_to(canonical_sum(u - pt - qt), (6, 128))
    send_all(message, jnp.concatenate([cross, first, second, total], axis=0))
    shifts[...] = jnp.concatenate([u, pt, qt, h_row], axis=0)


def weights(rows, columns, sub, lane):
    products = dot_nt(rows, columns)
    values = jnp.exp2(products * BETA + widen(sub, BLOCK) + lane)
    mass = jnp.sum(values, axis=1, keepdims=True)
    mixed = jnp.dot(values.astype(jnp.bfloat16), columns, preferred_element_type=jnp.float32)
    return mass, mixed


def term(rows, part, columns, sub, lane):
    mass, mixed = weights(rows, columns, sub[part], lane)
    return (rows.astype(jnp.float32) * mass - mixed).reshape(8, OWN, WIDTH)


SECOND = slice(HALF, BLOCK)
FIRST = slice(0, HALF)


def gradient(rows, part, cross, self_):
    return term(rows, part, *cross) - term(rows, part, *self_)


def half_gradients(ref, part, c_own, c_other, shifts, cols, out):
    x_col = block_rows(c_own, c_other, 0)
    y_col = block_rows(c_own, c_other, 1)
    u_sub, p_sub, q_sub, h_sub = [
        dense_to_sub(shifts[8 * k : 8 * k + 8, :]) for k in range(4)
    ]
    h_lane, u_lane, p_lane, q_lane = [
        dense_to_lane(cols[8 * k : 8 * k + 8, :]) - LOG_COUNT for k in range(4)
    ]
    rows = half_rows(ref, 0)
    out[:, 0:OWN, :] = gradient(rows, part, (y_col, u_sub, h_lane), (x_col, p_sub, p_lane))
    rows = half_rows(ref, 1)
    cross = term(rows, part, x_col, h_sub, u_lane)
    out[:, 2 * OWN : 3 * OWN, :] = cross
    out[:, OWN : 2 * OWN, :] = cross - term(rows, part, y_col, q_sub, q_lane)


def other_gradients(r_other, c_own, c_other, shifts, h_in, got, sent, cols, scale, sums):
    far = lax.axis_index("xh")
    change = LOG_COUNT - log2(join_sums(got, far, 0))
    h = h_in[...] + change
    u_col, p_col = unpair(*piggy_rows(got, 8, far))
    q_col, unused = unpair(*piggy_rows(got, 9, far))
    cols[...] = jnp.concatenate([h, u_col, p_col, q_col], axis=0)
    own_change = jnp.broadcast_to(own_piece(change, lax.axis_index("z")), (128, 128)).T
    scale[...] = widen(jnp.exp2(own_change[0:OWN, :]), WIDTH)
    total = jnp.sum(got[:, 8:16, :], axis=0)
    part = jnp.broadcast_to(canonical_sum(h), (8, 128))
    sums[...] = jnp.concatenate([jnp.broadcast_to(total[2:3], (8, 128)), part], axis=0)
    half_gradients(r_other, SECOND, c_own, c_other, shifts, cols, sent)


def own_gradients(r_own, c_own, c_other, shifts, cols, kept):
    half_gradients(r_own, FIRST, c_own, c_other, shifts, cols, kept)


def join_gradients(kept, back, sums, sum_back, out):
    for spot in range(8):
        side, y = spot // 4, spot % 4
        total = kept[spot : spot + 1] + back[spot : spot + 1]
        out[2 * y + side : 2 * y + side + 1, 0 : 3 * OWN, :] = total.astype(out.dtype)
    part = jnp.broadcast_to(sums[8:9, :] + sum_back[8:9, :], (16, 128))
    high = part.astype(jnp.bfloat16)
    left = part - high.astype(jnp.float32)
    middle = left.astype(jnp.bfloat16)
    low = left - middle.astype(jnp.float32)
    row = lax.broadcasted_iota(jnp.int32, (16, 128), 0)
    rest = jnp.where(row < 8, left, low).astype(jnp.bfloat16)
    tail = jnp.concatenate([high, rest], axis=1)
    out[:, 3 * OWN :, :] = jnp.broadcast_to(tail[None], (8, 16, WIDTH))


def finish(parts, scale, sums, grad_x, grad_y, divergence):
    summed = jnp.sum(parts[...].astype(jnp.float32), axis=0)
    grad_x[...] = summed[0:OWN]
    grad_y[...] = summed[OWN : 2 * OWN] + (scale[...] - 1.0) * summed[2 * OWN : 3 * OWN]
    high = summed[192:193, 0:128]
    whole = high + (summed[192:193, 128:256] + summed[200:201, 128:256])
    divergence[...] = (whole + sums[0:1, :])[0:1, 0:1] * (1.0 / (POINTS * BETA))


def call(body, outs, passes, *args):
    shapes = [jax.ShapeDtypeStruct(shape, dtype) for shape, dtype in outs]
    specs = [pl.BlockSpec(memory_space=pltpu.VMEM)] * len(args)
    return pl.pallas_call(
        body,
        out_shape=shapes,
        in_specs=specs,
        out_specs=[pl.BlockSpec(memory_space=pltpu.VMEM)] * len(outs),
        compiler_params=pltpu.CompilerParams(vmem_limit_bytes=VMEM_LIMIT),
        cost_estimate=pl.CostEstimate(
            flops=passes * 2 * BLOCK * BLOCK * WIDTH,
            bytes_accessed=4 * BLOCK * WIDTH * 2,
            transcendentals=passes * BLOCK * BLOCK,
        ),
    )(*args)


def share(message, axes, groups=None):
    return lax.all_to_all(message, axes, 0, 0, tiled=True, axis_index_groups=groups)


def share_col(message):
    groups = [
        [far * 16 + z * 2 + (side ^ far) for far in range(2) for z in range(8)] for side in range(2)
    ]
    return share(message, ("xh", "z", "xl"), groups)


def core_swap(values):
    return lax.ppermute(values, "core", [(0, 1), (1, 0)])


def pair_swap(values):
    return lax.ppermute(values, ("xh", "xl"), [(0, 3), (1, 2), (2, 1), (3, 0)])


def y_step(values, shift):
    return lax.ppermute(values, "y", [(y, (y + shift) % 4) for y in range(4)])


def on_device(regions, phrases):
    f32 = jnp.float32
    block = ((8, 2 * OWN, WIDTH), jnp.bfloat16)
    own = jnp.concatenate([regions, phrases], axis=0)
    (copies,) = call(
        spread, [((8, 3 * OWN, WIDTH), jnp.bfloat16)], 0, own, pair_swap(phrases)
    )
    c_own = share(copies, ("z",))
    near = jnp.stack([own] + [y_step(own, shift) for shift in (1, 2, 3)])
    across = lax.ppermute(near, "xl", [(0, 1), (1, 0)])
    near_far = core_swap(near)
    across_far = core_swap(across)

    def message(rows):
        return ((16, rows, 128), f32)

    sent, r_own, r_other = call(
        first_rows, [message(8), block, block], 1, near, across, near_far, across_far, c_own
    )
    c_regions = pair_swap(c_own[:, 0:OWN, :])
    later, sent = lax.optimization_barrier(((r_own, r_other, c_own), sent))
    got = share(sent, ROW_GROUP)
    sums, norms, c_other = call(
        first_self, [((16, 128), f32), ((32, 128), f32), block], 2, *later, c_regions
    )
    points = (r_own, r_other, c_own, c_other)
    sent, state = call(
        first_cols, [message(24), ((8, 128), f32)], 1, *points, sums, got
    )
    got = share_col(sent)
    sent, h_first = call(
        second_rows, [message(32), ((8, 128), f32)], 3, *points, norms, state, got
    )
    got = share(sent, ROW_GROUP)
    sent, shifts = call(
        second_cols,
        [message(16), ((32, 128), f32)],
        1,
        *points,
        norms,
        state,
        h_first,
        got,
    )
    got = share_col(sent)
    half = ((8, 3 * OWN, WIDTH), f32)
    away, cols, scale, sums = call(
        other_gradients,
        [half, ((32, 128), f32), ((OWN, WIDTH), f32), ((16, 128), f32)],
        2,
        *points[1:],
        shifts,
        h_first,
        got,
    )
    back, sum_back = core_swap(away), core_swap(sums)
    (kept,) = call(own_gradients, [half], 2, r_own, c_own, c_other, shifts, cols)
    (joined,) = call(
        join_gradients,
        [((8, 3 * OWN + 16, WIDTH), jnp.bfloat16)],
        0,
        kept,
        back,
        sums,
        sum_back,
    )
    grad_x, grad_y, divergence = call(
        finish,
        [((OWN, WIDTH), f32), ((OWN, WIDTH), f32), ((1, 1), f32)],
        0,
        share(joined, ("y", "xl")),
        scale,
        sums,
    )
    return (grad_x, grad_y, divergence[0, 0])


def solution(mesh):
    fine = Mesh(mesh.devices.reshape(2, 8, 2, 2, 4), AXES)
    return jax.shard_map(
        on_device,
        mesh=fine,
        in_specs=(P(AXES, None), P(AXES, None)),
        out_specs=(P(AXES, None), P(AXES, None), P()),
        check_vma=False,
    )
```
